1024 devices in a mesh: dom: 64 (over y, x), group: 16 (over z, core).
Axes of the slice: x: 8, y: 8, z: 8, core: 2. Of those that a mesh axis runs over, the one named last changes fastest.
Arguments:
- features: bfloat16 [16, 64, 512, 256], P('group', 'dom'), may hold values from -6 to 6
- new_owner: int32 [16, 64, 64, 1], P('group', 'dom'), may hold values from 0 to 63; in each aligned block of 64 rows (0 to 63, 64 to 127, ..., all dimensions but the last counted through in order) at most 2 rows name the same one
- rim_rows: int32 [16, 64, 4, 128], P('group', 'dom'), may hold values from 0 to 1023
- rim_counts: int32 [16, 64, 4], P('group', 'dom'), may hold values from 1 to 128, 256 in all within a row
- tile_sources: int32 [16, 64, 8, 4], P('group', 'dom'), may hold values from 0 to 11
- tile_values: bfloat16 [16, 64, 8, 4, 128, 128], P('group', 'dom'), may hold values from -0.25 to 0.25
- w_self: bfloat16 [256, 256], replicated, may hold values from -0.375 to 0.375
- w_neigh: bfloat16 [256, 256], replicated, may hold values from -0.375 to 0.375
- cotangent: bfloat16 [16, 64, 1024, 256], P('group', 'dom'), may hold values from -6 to 6
Outputs:
- layer_out: bfloat16 [16, 64, 1024, 256], P('group', 'dom')
- grad_self: float32 [256, 256], replicated
- grad_neigh: float32 [256, 256], replicated
The draws below stay inside these ranges and needn't reach their ends.
Inputs may be any that keep to these rules, and one draw needn't show every extreme that they name: `new_owner`: no device sends more than 2 blocks to one new owner; some device sends exactly 2 to one. `rim_rows`: slot p of device (g, d) goes to: p = 0 the next device along dom, p = 1 the previous along dom, p = 2 the next along group, p = 3 the previous along group. `rim_counts`: some peer of every device gets exactly 128 rows. `tile_sources`: tiles below 8 are the device's own; tile 8 holds slot 0 of the previous device along dom, tile 8 + 1 slot 1 of the next along dom, tile 8 + 2 slot 2 of the previous along group, tile 8 + 3 slot 3 of the next along group.
All inputs are finite; a program needn't handle non-finite values.
Results may differ from the reference program's by a relative error of at most 0.0061.
Values may be sent and summed in bfloat16 or wider, within the bound.
A program may use at most 32 MiB of HBM per device.

```python
import math
import jax
import jax.numpy as jnp
import numpy as np
from jax import lax

F = 256
H = 256
TILE = 128
RB = 8
TPR = 4
NB_DEV = 64
ROWS_DEV = 512
CAP = 2
LROWS = 1024
LT = 8
BND = 128
NODES = 524288
N_DOM = 64
N_GROUP = 16


def set_ends(values, own_key, smallest, largest):
    place = [jax.random.randint(jax.random.fold_in(own_key, axis), (), 0, length) for axis, length in enumerate(values.shape)]
    main_axis = values.shape.index(max(values.shape))
    next_to = place[:main_axis] + [(place[main_axis] + 1) % values.shape[main_axis]] + place[main_axis + 1:]
    return values.at[tuple(place)].set(smallest).at[tuple(next_to)].set(largest)


def block_scale(own_key, dims, split, low, largest):
    gain, own = 1.0, jax.random.fold_in(own_key, 6)
    for dim, parts in split:
        steps = jnp.exp(jax.random.uniform(jax.random.fold_in(own, dim), (parts,), jnp.float32, low / len(split), largest / len(split)))
        gain = gain * jnp.repeat(steps, dims[dim] // parts).reshape([-1 if axis == dim else 1 for axis in range(len(dims))])
    return gain


def length_profile(number_of, total, reach, lean):
    weights = [(1 << 20) // math.isqrt(rank ** lean) + 1 for rank in range(2, number_of + 1)]
    surplus, given = total - reach - (number_of - 1), [1] * (number_of - 1)
    while surplus > 0:
        free = [i for i in range(number_of - 1) if given[i] < reach]
        pool, budget = sum([weights[i] for i in free]), surplus
        for i in free:
            addition = min(reach - given[i], max(1, budget * weights[i] // pool), surplus)
            given[i] = given[i] + addition
            surplus = surplus - addition
    return np.array([reach] + given)


def ragged_sizes(own_key, count, total, most, lean):
    if count == 2:
        one = jax.random.randint(own_key, (), max(1, total - most), min(most, total - 1) + 1)
        return jnp.stack([one, total - one])
    sizes = jnp.asarray(length_profile(count, total, most, lean), jnp.int32)
    pairs = (count - 1) // 2
    giver, receiver = sizes[1:1 + 2 * pairs:2], sizes[2:2 + 2 * pairs:2]
    room = jnp.minimum(giver - 1, most - receiver)
    moved = jax.random.randint(jax.random.fold_in(own_key, 1), (pairs,), 0, 1 << 20) % (room + 1)
    sizes = sizes.at[1:1 + 2 * pairs:2].set(giver - moved).at[2:2 + 2 * pairs:2].set(receiver + moved)
    return sizes[jax.random.permutation(jax.random.fold_in(own_key, 2), count)]


def shared_out(stream_key, own, number, rows, number_of, top, limit, lean):
    order = jax.random.permutation(stream_key, number_of)
    crowded, ordinary = load_shares(number_of, rows * top, limit, lean, True), load_shares(number_of, rows * top, limit, lean, False)
    places = jnp.arange(number_of)

    def named(tallies, offset_by):
        used = int((tallies > 0).sum())
        fixed = max(1, used // 4)
        passed = fixed + (places - fixed + offset_by * (used - fixed)) % max(1, number_of - fixed)
        return jnp.zeros((number_of,), jnp.int32).at[order[jnp.where(places < fixed, places, passed)]].set(jnp.asarray(tallies, jnp.int32))

    tallies = jnp.where(number % 4 == 0, named(crowded, number // 4), named(ordinary, number - number // 4 - 1))
    mixed = jax.random.permutation(jax.random.fold_in(own, 3), number_of)
    donor, taker = mixed[0:number_of // 2 * 2:2], mixed[1:number_of // 2 * 2:2]
    slack = jnp.minimum(tallies[donor] - 1, limit - tallies[taker]) // 2
    slack = jnp.where((donor == order[0]) | (taker == order[0]) | (tallies[taker] == 0), 0, jnp.maximum(slack, 0))
    passed = jax.random.randint(jax.random.fold_in(own, 4), (number_of // 2,), 0, 1 << 20) % (slack + 1)
    tallies = tallies.at[donor].add(-passed).at[taker].add(passed)
    members = jnp.searchsorted(jnp.cumsum(tallies), jnp.arange(rows * top), side="right").astype(jnp.int32)
    listing = members.reshape(top, rows).T
    listing = listing[jax.random.permutation(jax.random.fold_in(own, 1), rows)]
    offset_by = jax.random.randint(jax.random.fold_in(own, 2), (rows, 1), 0, top)
    return jnp.take_along_axis(listing, (jnp.arange(top)[None, :] + offset_by) % top, axis=1)


def load_shares(count, total, reach, lean, full):
    portions = [(1 << 20) // math.isqrt(standing ** lean) + 1 for standing in range(1, count + 1)]
    largest = reach if full else min(reach, max(-(-total // count), total * portions[0] // sum(portions)))
    least = 1 if total - largest >= count - 1 else 0
    holding, spare = [largest] + [least] * (count - 1), total - largest - least * (count - 1)
    while spare > 0:
        candidates = [i for i in range(1, count) if holding[i] < largest] or [i for i in range(1, count) if holding[i] < reach]
        mass, budget = sum([portions[i] for i in candidates]), spare
        for i in candidates:
            more = min(reach - holding[i], max(1, budget * portions[i] // mass), spare)
            holding[i] = holding[i] + more
            spare = spare - more
    return np.array(holding)


def noise(key, dims, deviation, bound, cuts=(), kind=jnp.bfloat16):
    level = block_scale(key, dims, cuts, -0.22, 0.18) if cuts else 1.0
    result = jax.random.normal(key, dims, jnp.float32) * deviation * level
    return jnp.minimum(jnp.maximum(result, -bound), bound).astype(kind)


def setup_inputs(seed: int = 0) -> dict:
    key_list = jax.random.split(jax.random.key(seed), 10)
    features = noise(key_list[0], (N_GROUP, N_DOM, ROWS_DEV, F), 1.0, 6.0, ((0, 16), (1, 64)))
    new_owner_keys = jax.random.split(jax.random.fold_in(key_list[1], 1), N_GROUP * N_DOM * NB_DEV // NB_DEV)
    new_owner_turns = jax.random.permutation(jax.random.fold_in(key_list[1], 3), N_GROUP * N_DOM * NB_DEV // NB_DEV)
    new_owner = jax.vmap(lambda own, number: shared_out(jax.random.fold_in(key_list[1], 2), own, number, NB_DEV, N_DOM, 1, CAP, 2))(new_owner_keys, new_owner_turns).reshape((N_GROUP, N_DOM, NB_DEV, 1))
    rim_rows = set_ends(jax.random.randint(key_list[2], (N_GROUP, N_DOM, 4, BND), 0, LROWS), jax.random.fold_in(key_list[2], 1), 0, LROWS - 1).astype(jnp.int32)
    rim_counts = jax.vmap(lambda own: ragged_sizes(own, 4, 2 * BND, BND, 2))(jax.random.split(key_list[3], N_GROUP * N_DOM)).reshape((N_GROUP, N_DOM, 4)).astype(jnp.int32)
    tile_sources = set_ends(jax.random.randint(key_list[4], (N_GROUP, N_DOM, LT, TPR), 0, LT + 4), jax.random.fold_in(key_list[4], 1), 0, (LT + 4) - 1).astype(jnp.int32)
    tile_values = noise(key_list[5], (N_GROUP, N_DOM, LT, TPR, TILE, TILE), (TILE * TPR) ** -0.5, 0.25, ((0, 16), (1, 64)))
    w_self = noise(key_list[6], (F, H), F ** -0.5, 0.375)
    w_neigh = noise(key_list[7], (F, H), F ** -0.5, 0.375)
    cotangent = noise(key_list[8], (N_GROUP, N_DOM, LROWS, H), 1.0, 6.0, ((0, 16), (1, 64)))
    return {"features": features, "new_owner": new_owner, "rim_rows": rim_rows, "rim_counts": rim_counts, "tile_sources": tile_sources, "tile_values": tile_values, "w_self": w_self, "w_neigh": w_neigh, "cotangent": cotangent}


def reference(features, new_owner, rim_rows, rim_counts, tile_sources, tile_values, w_self, w_neigh, cotangent):
    groups, doms = (features.shape[0], features.shape[1])
    owner = new_owner[..., 0]
    order = jnp.arange(NB_DEV)
    earlier = order[None, :] < order[:, None]
    same = owner[..., :, None] == owner[..., None, :]
    rank = lax.optimization_barrier(jnp.sum(jnp.where(same & earlier, 1, 0), axis=-1)).astype(jnp.int32)
    blocks = features.reshape(groups, doms, NB_DEV, RB * F)
    gidx = jnp.arange(groups).astype(jnp.int32)[:, None, None]
    sidx = jnp.arange(doms).astype(jnp.int32)[None, :, None]
    owned = jnp.zeros((groups, doms, doms * CAP, RB * F), jnp.bfloat16)
    owned = owned.at[gidx, owner, sidx * CAP + rank].set(blocks)
    owned = owned.reshape(groups, doms, LROWS, F)
    picked = jax.vmap(jax.vmap(lambda a, i: a[i]))(owned, rim_rows)
    valid = jnp.arange(BND)[None, None, None, :] < rim_counts[..., None]
    sent = jnp.where(valid[..., None], picked, jnp.zeros_like(picked))
    recv0 = jnp.roll(sent[:, :, 0], 1, axis=1)
    recv1 = jnp.roll(sent[:, :, 1], -1, axis=1)
    recv2 = jnp.roll(sent[:, :, 2], 1, axis=0)
    recv3 = jnp.roll(sent[:, :, 3], -1, axis=0)
    ext_all = jnp.concatenate([owned, recv0, recv1, recv2, recv3], axis=2)
    total = groups * doms

    def device_step(carry, items):
        ext, sources, values, cot = items
        own_rows = ext[:LROWS]
        tiles = ext.reshape(LT + 4, TILE, F)
        chosen = jnp.take(tiles, sources, axis=0)
        summed = jnp.einsum('itab,itbf->iaf', values.astype(jnp.float32), chosen.astype(jnp.float32))
        neigh = summed.reshape(LROWS, F).astype(jnp.bfloat16)
        pre = jnp.dot(own_rows, w_self, preferred_element_type=jnp.float32) + jnp.dot(neigh, w_neigh, preferred_element_type=jnp.float32)
        sig = jax.nn.sigmoid(pre)
        out_rows = (pre * sig).astype(jnp.bfloat16)
        dpre = (cot.astype(jnp.float32) * sig * (1.0 + pre * (1.0 - sig))).astype(jnp.bfloat16)
        g_self = jnp.dot(own_rows.T, dpre, preferred_element_type=jnp.float32)
        g_neigh = jnp.dot(neigh.T, dpre, preferred_element_type=jnp.float32)
        return ((carry[0] + g_self, carry[1] + g_neigh), out_rows)
    zero = jnp.zeros((F, H), jnp.float32)
    items = (ext_all.reshape(total, LROWS + 4 * BND, F), tile_sources.reshape(total, LT, TPR), tile_values.reshape(total, LT, TPR, TILE, TILE), cotangent.reshape(total, LROWS, H))
    sums, outs = lax.scan(device_step, (zero, zero), items)
    scale = 1.0 / jnp.sqrt(jnp.float32(NODES))
    layer_out = outs.reshape(groups, doms, LROWS, H)
    return (layer_out, sums[0] * scale, sums[1] * scale)
```

```python
import functools
import math

import jax
import jax.numpy as jnp
from jax import lax
from jax.experimental import pallas as pl
from jax.experimental.pallas import tpu as pltpu
from jax.sharding import PartitionSpec as P

F32 = jnp.float32
BF16 = jnp.bfloat16
I32 = jnp.int32
SIDE = 8
TILE = 128
RB = 8
CONTRACT_ROWS = (((0,), (0,)), ((), ()))


def iota(shape, axis):
    return lax.broadcasted_iota(I32, shape, axis)


def to_column(row, n):
    grid = jnp.where(iota((n, n), 0) == iota((n, n), 1), jnp.broadcast_to(row, (n, n)), 0)
    return jnp.sum(grid, axis=1, keepdims=True)


def kernel(
    scale,
    feat_hbm,
    owner_hbm,
    rim_hbm,
    cnt_hbm,
    src_hbm,
    val_hbm,
    ws_hbm,
    wn_hbm,
    cot_hbm,
    out_hbm,
    gs_hbm,
    gn_hbm,
    feat,
    owner,
    rim,
    cnt,
    src,
    val,
    ws,
    wn,
    cot,
    out,
    outbox,
    ext,
    pick,
    rim_out,
    x_t,
    pre_self,
    dpre,
    g_out,
    g_in,
    part,
    recv_a,
    red_a,
    recv_b,
    recv_z,
    recv_c,
    gat_b,
    gat_a,
    total,
    grad,
    in_sems,
    out_sems,
    a2a_send,
    a2a_recv,
    rim_send,
    rim_recv,
    ph_send,
    ph_recv,
):
    dom = lax.axis_index("dom")
    group = lax.axis_index("group")
    my_x, my_y = lax.rem(dom, SIDE), lax.div(dom, SIDE)
    my_z, core = lax.div(group, 2), lax.rem(group, 2)
    peers = SIDE * SIDE
    n_group = 2 * SIDE
    other = group + 1 - 2 * core

    loads = []
    for k, (a, b) in enumerate(
        (
            (owner_hbm, owner),
            (feat_hbm, feat),
            (rim_hbm, rim),
            (cnt_hbm, cnt),
            (src_hbm, src),
            (ws_hbm, ws),
            (wn_hbm, wn),
            (val_hbm, val),
            (cot_hbm, cot),
        )
    ):
        loads.append(pltpu.make_async_copy(a, b, in_sems.at[k]))
        loads[-1].start()
    l_owner, l_feat, l_rim, l_cnt, l_src, l_ws, l_wn, l_val, l_cot = loads

    barrier = pltpu.get_barrier_semaphore()

    def greet_dom(i, c):
        pl.semaphore_signal(
            barrier, inc=1, device_id={"dom": lax.rem(dom + i, peers), "group": group}
        )
        return c

    lax.fori_loop(1, peers, greet_dom, 0)

    def greet_z(i, c):
        pl.semaphore_signal(
            barrier,
            inc=1,
            device_id={"dom": dom, "group": lax.rem(my_z + i, SIDE) * 2 + core},
        )
        return c

    lax.fori_loop(1, SIDE, greet_z, 0)
    group_next = lax.rem(group + 1, n_group)
    group_prev = lax.rem(group + n_group - 1, n_group)
    for g in (group_next, group_prev):
        pl.semaphore_signal(barrier, inc=1, device_id={"dom": dom, "group": g})

    blocks = owner.shape[1]
    rows = feat.shape[0]
    l_owner.wait()
    owner_col = to_column(owner[...], blocks)
    block_of = lax.div(iota((blocks, rows), 1), RB)
    block_id = iota((blocks, rows), 0)
    owner_b = jnp.broadcast_to(owner_col, (blocks, rows))
    owner_row = jnp.sum(jnp.where(block_id == block_of, owner_b, 0), axis=0, keepdims=True)
    before = (owner_b == jnp.broadcast_to(owner_row, (blocks, rows))) & (block_id < block_of)
    rank = jnp.sum(jnp.where(before, 1, 0), axis=0, keepdims=True)
    slot_row = (owner_row * 2 + rank) * RB + lax.rem(iota((1, rows), 1), RB)

    l_feat.wait()
    share = 2 * RB
    for j in range(SIDE):
        yj = lax.rem(my_y + j, SIDE)
        hot = jnp.where(
            iota((TILE, rows), 0) + yj * TILE == jnp.broadcast_to(slot_row, (TILE, rows)),
            1.0,
            0.0,
        ).astype(BF16)
        outbox[yj] = jnp.dot(hot, feat[...], preferred_element_type=F32).astype(BF16)
        if j == 0:
            pl.semaphore_wait(barrier, peers - 1 + SIDE - 1 + 2)
            mine = pltpu.make_async_copy(
                outbox.at[my_y, pl.ds(my_x * share, share)],
                ext.at[my_y, pl.ds(my_x * share, share)],
                a2a_recv,
            )
            mine.start()

        def send(i, c, yj=yj):
            xi = lax.rem(my_x + i, SIDE)
            pltpu.make_async_remote_copy(
                src_ref=outbox.at[yj, pl.ds(xi * share, share)],
                dst_ref=ext.at[my_y, pl.ds(my_x * share, share)],
                send_sem=a2a_send,
                recv_sem=a2a_recv,
                device_id={"dom": yj * SIDE + xi, "group": group},
            ).start()
            return c

        lax.fori_loop(1 if j == 0 else 0, SIDE, send, 0)

    l_rim.wait()
    l_cnt.wait()
    n_rows = SIDE * TILE
    for p in range(4):
        column = to_column(rim[p : p + 1, :], TILE)
        column = jnp.where(iota((TILE, 1), 0) < cnt[0, p], column, -1)
        pick[p] = jnp.where(
            iota((TILE, n_rows), 1) == jnp.broadcast_to(column, (TILE, n_rows)), 1.0, 0.0
        ).astype(BF16)
    l_ws.wait()
    l_wn.wait()
    l_src.wait()
    l_val.wait()
    l_cot.wait()

    whole = ext.at[pl.ds(0, SIDE)]
    pltpu.make_async_copy(whole, whole, a2a_recv).wait()

    rims = (
        (0, {"dom": lax.rem(dom + 1, peers), "group": group}),
        (1, {"dom": lax.rem(dom + peers - 1, peers), "group": group}),
        (2, {"dom": dom, "group": group_next}),
        (3, {"dom": dom, "group": group_prev}),
    )
    owned = ext[0:SIDE].reshape(n_rows, feat.shape[1])
    rim_copies = []
    for p, target in rims:
        rim_out[p] = jnp.dot(pick[p], owned, preferred_element_type=F32).astype(BF16)
        rim_copies.append(
            pltpu.make_async_remote_copy(
                src_ref=rim_out.at[p],
                dst_ref=ext.at[SIDE + p],
                send_sem=rim_send.at[p],
                recv_sem=rim_recv.at[p],
                device_id=target,
            )
        )
        rim_copies[-1].start()
    for i in range(SIDE):
        tile = ext[i]
        x_t[0, :, i * TILE : (i + 1) * TILE] = tile.T
        pre_self[i] = jnp.dot(tile, ws[...], preferred_element_type=F32)
    for copy in rim_copies:
        copy.wait_recv()

    stores = []
    for i in range(SIDE):
        lhs = jnp.concatenate([val[i, t] for t in range(4)], axis=1)
        rhs = jnp.concatenate([ext[src[t, i]] for t in range(4)], axis=0)
        neigh = jnp.dot(lhs, rhs, preferred_element_type=F32).astype(BF16)
        x_t[1, :, i * TILE : (i + 1) * TILE] = neigh.T
        pre = pre_self[i] + jnp.dot(neigh, wn[...], preferred_element_type=F32)
        sig = jax.nn.sigmoid(pre)
        out[pl.ds(i * TILE, TILE), :] = (pre * sig).astype(BF16)
        dpre[pl.ds(i * TILE, TILE), :] = (
            cot[pl.ds(i * TILE, TILE), :].astype(F32) * sig * (1.0 + pre * (1.0 - sig))
        ).astype(BF16)
    store = pltpu.make_async_copy(out, out_hbm, out_sems.at[0])
    store.start()

    width = feat.shape[1]
    g_out[...] = jnp.dot(x_t[1 - core], dpre[...], preferred_element_type=F32)
    pair = pltpu.make_async_remote_copy(
        src_ref=g_out,
        dst_ref=g_in,
        send_sem=ph_send.at[0],
        recv_sem=ph_recv.at[0],
        device_id={"dom": dom, "group": other},
    )
    pair.start()
    own = jnp.dot(x_t[core], dpre[...], preferred_element_type=F32)
    pair.wait_recv()
    piece = width // SIDE
    part[...] = (own + g_in[...]).reshape(SIDE, piece, width)

    a, b = my_x + core * (my_y - my_x), my_y + core * (my_x - my_y)
    step_a, step_b = 1 + core * (SIDE - 1), SIDE - core * (SIDE - 1)

    def along(axis, k):
        if axis == "a":
            return {"dom": k * step_a + b * step_b, "group": group}
        if axis == "b":
            return {"dom": a * step_a + k * step_b, "group": group}
        return {"dom": dom, "group": k * 2 + core}

    def exchange(axis, me, phase, source, target):
        pltpu.make_async_copy(source(me), target.at[me], ph_recv.at[phase]).start()

        def send(i, c):
            k = lax.rem(me + i, SIDE)
            pltpu.make_async_remote_copy(
                src_ref=source(k),
                dst_ref=target.at[me],
                send_sem=ph_send.at[phase],
                recv_sem=ph_recv.at[phase],
                device_id=along(axis, k),
            ).start()
            return c

        lax.fori_loop(1, SIDE, send, 0)
        pltpu.make_async_copy(target, target, ph_recv.at[phase]).wait()

    exchange("a", a, 1, lambda k: part.at[k], recv_a)
    summed = jnp.sum(recv_a[...], axis=0)
    for k in range(SIDE):
        red_a[k] = summed[k // 2 * 8 : k // 2 * 8 + 8, k % 2 * TILE : k % 2 * TILE + TILE]
    exchange("b", b, 2, lambda k: red_a.at[k], recv_b)
    recv_c[...] = jnp.sum(recv_b[...], axis=0)
    exchange("z", my_z, 3, lambda k: recv_c, recv_z)
    recv_c2 = jnp.sum(recv_z[...], axis=0) * scale
    total[...] = recv_c2
    exchange("b", b, 4, lambda k: total, gat_b)
    exchange("a", a, 5, lambda k: gat_b, gat_a.at[core])
    back = pltpu.make_async_remote_copy(
        src_ref=gat_a.at[core],
        dst_ref=gat_a.at[core],
        send_sem=ph_send.at[6],
        recv_sem=ph_recv.at[6],
        device_id={"dom": dom, "group": other},
    )
    back.start()
    back.wait_recv()
    for w in range(2):
        for i in range(SIDE):
            for k in range(SIDE):
                r = i * piece + k // 2 * 8
                grad[w, r : r + 8, k % 2 * TILE : k % 2 * TILE + TILE] = gat_a[w, i, k]
    finals = [
        pltpu.make_async_copy(grad.at[0], gs_hbm, out_sems.at[1]),
        pltpu.make_async_copy(grad.at[1], gn_hbm, out_sems.at[2]),
    ]
    for copy in finals:
        copy.start()

    sent = outbox.at[pl.ds(0, SIDE - 1)]
    pltpu.make_async_copy(sent, sent, a2a_send).wait()
    rest = outbox.at[0, pl.ds(0, (SIDE - 1) * share)]
    pltpu.make_async_copy(rest, rest, a2a_send).wait()
    for copy in rim_copies:
        copy.wait_send()
    pair.wait_send()
    for phase, like in (
        (1, recv_a),
        (2, recv_b),
        (3, recv_z),
        (4, gat_b),
        (5, gat_a.at[0]),
    ):
        seven = like.at[pl.ds(0, SIDE - 1)]
        pltpu.make_async_copy(seven, seven, ph_send.at[phase]).wait()
    back.wait_send()
    store.wait()
    for copy in finals:
        copy.wait()


def on_device(
    features, new_owner, rim_rows, rim_counts, tile_sources, tile_values, w_self, w_neigh, cotangent
):
    rows, width = features.shape[2:]
    blocks = new_owner.shape[2]
    n_rows = cotangent.shape[2]
    hid = w_self.shape[1]
    nodes = rows * lax.axis_size("dom") * lax.axis_size("group")
    scale = 1.0 / math.sqrt(nodes)
    any_spec = pl.BlockSpec(memory_space=pl.ANY)
    out, g_self, g_neigh = pl.pallas_call(
        functools.partial(kernel, scale),
        out_shape=(
            jax.ShapeDtypeStruct((n_rows, hid), BF16),
            jax.ShapeDtypeStruct((width, hid), F32),
            jax.ShapeDtypeStruct((width, hid), F32),
        ),
        in_specs=[any_spec] * 9,
        out_specs=[any_spec] * 3,
        scratch_shapes=[
            pltpu.VMEM((rows, width), BF16),
            pltpu.VMEM((1, blocks), I32),
            pltpu.VMEM((4, TILE), I32),
            pltpu.SMEM((1, 4), I32),
            pltpu.SMEM((4, SIDE), I32),
            pltpu.VMEM((SIDE, 4, TILE, TILE), BF16),
            pltpu.VMEM((width, hid), BF16),
            pltpu.VMEM((width, hid), BF16),
            pltpu.VMEM((n_rows, hid), BF16),
            pltpu.VMEM((n_rows, hid), BF16),
            pltpu.VMEM((SIDE, TILE, width), BF16),
            pltpu.VMEM((SIDE + 4, TILE, width), BF16),
            pltpu.VMEM((4, TILE, n_rows), BF16),
            pltpu.VMEM((4, TILE, width), BF16),
            pltpu.VMEM((2, width, n_rows), BF16),
            pltpu.VMEM((SIDE, TILE, hid), F32),
            pltpu.VMEM((n_rows, hid), BF16),
            pltpu.VMEM((width, hid), F32),
            pltpu.VMEM((width, hid), F32),
            pltpu.VMEM((SIDE, width // SIDE, hid), F32),
            pltpu.VMEM((SIDE, width // SIDE, hid), F32),
            pltpu.VMEM((SIDE, 8, TILE), F32),
            pltpu.VMEM((SIDE, 8, TILE), F32),
            pltpu.VMEM((SIDE, 8, TILE), F32),
            pltpu.VMEM((8, TILE), F32),
            pltpu.VMEM((SIDE, 8, TILE), F32),
            pltpu.VMEM((2, SIDE, SIDE, 8, TILE), F32),
            pltpu.VMEM((8, TILE), F32),
            pltpu.VMEM((2, width, hid), F32),
            pltpu.SemaphoreType.DMA((9,)),
            pltpu.SemaphoreType.DMA((3,)),
            pltpu.SemaphoreType.DMA,
            pltpu.SemaphoreType.DMA,
            pltpu.SemaphoreType.DMA((4,)),
            pltpu.SemaphoreType.DMA((4,)),
            pltpu.SemaphoreType.DMA((7,)),
            pltpu.SemaphoreType.DMA((7,)),
        ],
        compiler_params=pltpu.CompilerParams(
            collective_id=0, has_side_effects=True, vmem_limit_bytes=48 * 1024 * 1024
        ),
    )(
        features[0, 0],
        new_owner[0, 0, :, 0][None],
        rim_rows[0, 0],
        rim_counts[0],
        tile_sources[0, 0].T,
        tile_values[0, 0],
        w_self,
        w_neigh,
        cotangent[0, 0],
    )
    return (out[None, None], g_self, g_neigh)


def solution(mesh):
    return jax.shard_map(
        on_device,
        mesh=mesh,
        in_specs=(
            P("group", "dom", None, None),
            P("group", "dom", None, None),
            P("group", "dom", None, None),
            P("group", "dom", None),
            P("group", "dom", None, None),
            P("group", "dom", None, None, None, None),
            P(),
            P(),
            P("group", "dom", None, None),
        ),
        out_specs=(P("group", "dom", None, None), P(), P()),
        check_vma=False,
    )
```

```python
import functools
import math

import jax
import jax.numpy as jnp
from jax import lax
from jax.experimental import pallas as pl
from jax.experimental.pallas import tpu as pltpu
from jax.sharding import PartitionSpec as P

F32 = jnp.float32
BF16 = jnp.bfloat16
I32 = jnp.int32
SIDE = 8
TILE = 128
RB = 8
PIECES = SIDE * SIDE // 2
Z_STEPS = (4, 3, 5, 2, 6, 1, 7)
VMEM_LIMIT = 48 * 1024 * 1024


def ring(d):
    return min(d, SIDE - d)


STEPS = sorted(
    ((dx, dy) for dy in range(SIDE) for dx in range(SIDE) if dx or dy),
    key=lambda s: -ring(s[0]) - ring(s[1]),
)
EVEN = [s for s in STEPS if sum(s) % 2 == 0] + [(0, 0)]
ODD = [s for s in STEPS if sum(s) % 2 == 1]


def iota(shape, axis):
    return lax.broadcasted_iota(I32, shape, axis)


def to_column(row, n):
    grid = jnp.where(iota((n, n), 0) == iota((n, n), 1), jnp.broadcast_to(row, (n, n)), 0)
    return jnp.sum(grid, axis=1, keepdims=True)


def kernel(
    scale,
    feat_hbm,
    owner_hbm,
    rim_hbm,
    cnt_hbm,
    src_hbm,
    val_hbm,
    ws_hbm,
    wn_hbm,
    cot_hbm,
    out_any,
    gath,
    feat,
    owner,
    rim,
    cnt,
    src,
    val,
    ws,
    wn,
    cot,
    out,
    outbox,
    ext,
    pick,
    rim_out,
    x_t,
    pre_self,
    dpre,
    g_out,
    g_in,
    part,
    recv,
    z_part,
    recv_z,
    total,
    in_sems,
    out_sem,
    a2a_send,
    a2a_recv,
    rim_send,
    rim_recv,
    ph_send,
    ph_recv,
):
    dom = lax.axis_index("dom")
    group = lax.axis_index("group")
    my_x, my_y = lax.rem(dom, SIDE), lax.div(dom, SIDE)
    my_z, core = lax.div(group, 2), lax.rem(group, 2)
    peers = SIDE * SIDE
    n_group = 2 * SIDE
    other = group + 1 - 2 * core

    pending = []

    def wait_for(like, sem):
        pltpu.make_async_copy(like, like, sem).wait()

    loads = []
    for k, (a, b) in enumerate(
        (
            (owner_hbm, owner),
            (feat_hbm, feat),
            (rim_hbm, rim),
            (cnt_hbm, cnt),
            (src_hbm, src),
            (ws_hbm, ws),
            (wn_hbm, wn),
            (val_hbm, val),
            (cot_hbm, cot),
        )
    ):
        loads.append(pltpu.make_async_copy(a, b, in_sems.at[k]))
        loads[-1].start()
    l_owner, l_feat, l_rim, l_cnt, l_src, l_ws, l_wn, l_val, l_cot = loads

    barrier = pltpu.get_barrier_semaphore()

    def greet_dom(i, c):
        pl.semaphore_signal(
            barrier, inc=1, device_id={"dom": lax.rem(dom + i, peers), "group": group}
        )
        return c

    lax.fori_loop(1, peers, greet_dom, 0)

    def greet_z(i, c):
        pl.semaphore_signal(
            barrier,
            inc=1,
            device_id={"dom": dom, "group": lax.rem(my_z + i, SIDE) * 2 + core},
        )
        return c

    lax.fori_loop(1, SIDE, greet_z, 0)
    group_next = lax.rem(group + 1, n_group)
    group_prev = lax.rem(group + n_group - 1, n_group)
    for g in (group_next, group_prev):
        pl.semaphore_signal(barrier, inc=1, device_id={"dom": dom, "group": g})

    blocks = owner.shape[1]
    rows = feat.shape[0]
    l_owner.wait()
    owner_col = to_column(owner[...], blocks)
    block_of = lax.div(iota((blocks, rows), 1), RB)
    block_id = iota((blocks, rows), 0)
    owner_b = jnp.broadcast_to(owner_col, (blocks, rows))
    owner_row = jnp.sum(jnp.where(block_id == block_of, owner_b, 0), axis=0, keepdims=True)
    before = (owner_b == jnp.broadcast_to(owner_row, (blocks, rows))) & (block_id < block_of)
    rank = jnp.sum(jnp.where(before, 1, 0), axis=0, keepdims=True)
    slot_row = (owner_row * 2 + rank) * RB + lax.rem(iota((1, rows), 1), RB)

    l_feat.wait()
    share = 2 * RB
    for j in range(SIDE):
        hot = jnp.where(
            iota((TILE, rows), 0) + j * TILE == jnp.broadcast_to(slot_row, (TILE, rows)),
            1.0,
            0.0,
        ).astype(BF16)
        outbox[j] = jnp.dot(hot, feat[...], preferred_element_type=F32).astype(BF16)
    pl.semaphore_wait(barrier, peers - 1 + SIDE - 1 + 2)
    for dx, dy in STEPS:
        xi, yi = lax.rem(my_x + dx, SIDE), lax.rem(my_y + dy, SIDE)
        pltpu.make_async_remote_copy(
            src_ref=outbox.at[yi, pl.ds(xi * share, share)],
            dst_ref=ext.at[my_y, pl.ds(my_x * share, share)],
            send_sem=a2a_send,
            recv_sem=a2a_recv,
            device_id={"dom": yi * SIDE + xi, "group": group},
        ).start()
    pltpu.make_async_copy(
        outbox.at[my_y, pl.ds(my_x * share, share)],
        ext.at[my_y, pl.ds(my_x * share, share)],
        a2a_recv,
    ).start()
    pending.append(lambda: wait_for(outbox.at[pl.ds(0, SIDE - 1)], a2a_send))
    pending.append(lambda: wait_for(outbox.at[0, pl.ds(0, (SIDE - 1) * share)], a2a_send))

    l_rim.wait()
    l_cnt.wait()
    n_rows = SIDE * TILE
    for p in range(4):
        column = to_column(rim[p : p + 1, :], TILE)
        column = jnp.where(iota((TILE, 1), 0) < cnt[0, p], column, -1)
        pick[p] = jnp.where(
            iota((TILE, n_rows), 1) == jnp.broadcast_to(column, (TILE, n_rows)), 1.0, 0.0
        ).astype(BF16)
    l_ws.wait()
    l_wn.wait()
    l_src.wait()
    l_val.wait()
    l_cot.wait()

    wait_for(ext.at[pl.ds(0, SIDE)], a2a_recv)

    rims = (
        (0, {"dom": lax.rem(dom + 1, peers), "group": group}),
        (1, {"dom": lax.rem(dom + peers - 1, peers), "group": group}),
        (2, {"dom": dom, "group": group_next}),
        (3, {"dom": dom, "group": group_prev}),
    )
    owned = ext[0:SIDE].reshape(n_rows, feat.shape[1])
    rim_copies = []
    for p, target in rims:
        rim_out[p] = jnp.dot(pick[p], owned, preferred_element_type=F32).astype(BF16)
        rim_copies.append(
            pltpu.make_async_remote_copy(
                src_ref=rim_out.at[p],
                dst_ref=ext.at[SIDE + p],
                send_sem=rim_send.at[p],
                recv_sem=rim_recv.at[p],
                device_id=target,
            )
        )
        rim_copies[-1].start()
        pending.append(rim_copies[-1].wait_send)
    for i in range(SIDE):
        tile = ext[i]
        x_t[0, :, i * TILE : (i + 1) * TILE] = tile.T
        pre_self[i] = jnp.dot(tile, ws[...], preferred_element_type=F32)
    for copy in rim_copies:
        copy.wait_recv()

    stores = []
    for i in range(SIDE):
        lhs = jnp.concatenate([val[i, t] for t in range(4)], axis=1)
        rhs = jnp.concatenate([ext[src[t, i]] for t in range(4)], axis=0)
        neigh = jnp.dot(lhs, rhs, preferred_element_type=F32).astype(BF16)
        x_t[1, :, i * TILE : (i + 1) * TILE] = neigh.T
        pre = pre_self[i] + jnp.dot(neigh, wn[...], preferred_element_type=F32)
        sig = jax.nn.sigmoid(pre)
        out[pl.ds(i * TILE, TILE), :] = (pre * sig).astype(BF16)
        dpre[pl.ds(i * TILE, TILE), :] = (
            cot[pl.ds(i * TILE, TILE), :].astype(F32) * sig * (1.0 + pre * (1.0 - sig))
        ).astype(BF16)
    store = pltpu.make_async_copy(out, out_any, out_sem)
    store.start()
    pending.append(store.wait)

    width = feat.shape[1]
    g_out[...] = jnp.dot(x_t[1 - core], dpre[...], preferred_element_type=F32)
    pair = pltpu.make_async_remote_copy(
        src_ref=g_out,
        dst_ref=g_in,
        send_sem=ph_send.at[0],
        recv_sem=ph_recv.at[0],
        device_id={"dom": dom, "group": other},
    )
    pair.start()
    pending.append(pair.wait_send)
    own = jnp.dot(x_t[core], dpre[...], preferred_element_type=F32)
    pair.wait_recv()
    summed = own + g_in[...]
    for k in range(PIECES):
        r, c = k // 2 * 16, k % 2 * TILE
        part[k] = summed[r : r + 16, c : c + TILE].astype(BF16)

    odd = lax.rem(my_x + my_y + core, 2)
    mine = my_y * (SIDE // 2) + lax.div(my_x, 2)

    def to_owner(dx, dy):
        xi, yi = lax.rem(my_x + dx, SIDE), lax.rem(my_y + dy, SIDE)
        return pltpu.make_async_remote_copy(
            src_ref=part.at[yi * (SIDE // 2) + lax.div(xi, 2)],
            dst_ref=recv.at[dom],
            send_sem=ph_send.at[1],
            recv_sem=ph_recv.at[1],
            device_id={"dom": yi * SIDE + xi, "group": group},
        )

    for (ex, ey), (ox, oy) in zip(EVEN[:-1], ODD[:-1]):
        to_owner(ex + odd * (ox - ex), ey + odd * (oy - ey)).start()

    @pl.when(odd == 1)
    def _():
        to_owner(*ODD[-1]).start()

    @pl.when(odd == 0)
    def _():
        pltpu.make_async_copy(part.at[mine], recv.at[dom], ph_recv.at[1]).start()
        wait_for(recv, ph_recv.at[1])
        z_part[...] = jnp.sum(recv[...].astype(F32), axis=0)

        for i in Z_STEPS:
            pltpu.make_async_remote_copy(
                src_ref=z_part,
                dst_ref=recv_z.at[my_z],
                send_sem=ph_send.at[2],
                recv_sem=ph_recv.at[2],
                device_id={"dom": dom, "group": lax.rem(my_z + i, SIDE) * 2 + core},
            ).start()
        pltpu.make_async_copy(z_part, recv_z.at[my_z], ph_recv.at[2]).start()
        wait_for(recv_z, ph_recv.at[2])
        total[...] = (jnp.sum(recv_z[...], axis=0) * scale).astype(BF16)

        for dx, dy in STEPS:
            xi, yi = lax.rem(my_x + dx, SIDE), lax.rem(my_y + dy, SIDE)
            pltpu.make_async_remote_copy(
                src_ref=total,
                dst_ref=gath.at[core, mine],
                send_sem=ph_send.at[3],
                recv_sem=ph_recv.at[3],
                device_id={"dom": yi * SIDE + xi, "group": group},
            ).start()
        pltpu.make_async_copy(total, gath.at[core, mine], ph_recv.at[3]).start()

    wait_for(gath.at[core], ph_recv.at[3])
    back = pltpu.make_async_remote_copy(
        src_ref=gath.at[core],
        dst_ref=gath.at[core],
        send_sem=ph_send.at[4],
        recv_sem=ph_recv.at[4],
        device_id={"dom": dom, "group": other},
    )
    back.start()

    @pl.when(odd == 1)
    def _():
        wait_for(recv.at[pl.ds(0, PIECES)], ph_send.at[1])

    @pl.when(odd == 0)
    def _():
        wait_for(recv.at[pl.ds(0, PIECES - 1)], ph_send.at[1])
        wait_for(recv_z.at[pl.ds(0, SIDE - 1)], ph_send.at[2])
        wait_for(recv.at[pl.ds(0, peers - 1)], ph_send.at[3])

    for wait in pending:
        wait()
    back.wait()


def finish(out_in, gath, out, g_self, g_neigh, grads, sems):
    copies = [pltpu.make_async_copy(out_in, out, sems.at[2])]
    copies[0].start()
    for w, target in enumerate((g_self, g_neigh)):
        for k in range(PIECES):
            r, c = k // 2 * 16, k % 2 * TILE
            grads[w, r : r + 16, c : c + TILE] = gath[w, k].astype(F32)
        copies.append(pltpu.make_async_copy(grads.at[w], target, sems.at[w]))
        copies[-1].start()
    for copy in copies:
        copy.wait()


def on_device(
    features, new_owner, rim_rows, rim_counts, tile_sources, tile_values, w_self, w_neigh, cotangent
):
    rows, width = features.shape[2:]
    blocks = new_owner.shape[2]
    n_rows = cotangent.shape[2]
    hid = w_self.shape[1]
    nodes = rows * lax.axis_size("dom") * lax.axis_size("group")
    scale = 1.0 / math.sqrt(nodes)
    any_spec = pl.BlockSpec(memory_space=pl.ANY)
    out, gath = pl.pallas_call(
        functools.partial(kernel, scale),
        out_shape=(
            pltpu.VMEM((n_rows, hid), BF16),
            pltpu.VMEM((2, PIECES, 16, TILE), BF16),
        ),
        in_specs=[any_spec] * 9,
        out_specs=[any_spec] * 2,
        scratch_shapes=[
            pltpu.VMEM((rows, width), BF16),
            pltpu.VMEM((1, blocks), I32),
            pltpu.VMEM((4, TILE), I32),
            pltpu.SMEM((1, 4), I32),
            pltpu.SMEM((4, SIDE), I32),
            pltpu.VMEM((SIDE, 4, TILE, TILE), BF16),
            pltpu.VMEM((width, hid), BF16),
            pltpu.VMEM((width, hid), BF16),
            pltpu.VMEM((n_rows, hid), BF16),
            pltpu.VMEM((n_rows, hid), BF16),
            pltpu.VMEM((SIDE, TILE, width), BF16),
            pltpu.VMEM((SIDE + 4, TILE, width), BF16),
            pltpu.VMEM((4, TILE, n_rows), BF16),
            pltpu.VMEM((4, TILE, width), BF16),
            pltpu.VMEM((2, width, n_rows), BF16),
            pltpu.VMEM((SIDE, TILE, hid), F32),
            pltpu.VMEM((n_rows, hid), BF16),
            pltpu.VMEM((width, hid), F32),
            pltpu.VMEM((width, hid), F32),
            pltpu.VMEM((PIECES, 16, TILE), BF16),
            pltpu.VMEM((SIDE * SIDE, 16, TILE), BF16),
            pltpu.VMEM((16, TILE), F32),
            pltpu.VMEM((SIDE, 16, TILE), F32),
            pltpu.VMEM((16, TILE), BF16),
            pltpu.SemaphoreType.DMA((9,)),
            pltpu.SemaphoreType.DMA,
            pltpu.SemaphoreType.DMA,
            pltpu.SemaphoreType.DMA,
            pltpu.SemaphoreType.DMA((4,)),
            pltpu.SemaphoreType.DMA((4,)),
            pltpu.SemaphoreType.DMA((5,)),
            pltpu.SemaphoreType.DMA((5,)),
        ],
        compiler_params=pltpu.CompilerParams(
            collective_id=0, has_side_effects=True, vmem_limit_bytes=VMEM_LIMIT
        ),
    )(
        *(
            pltpu.with_memory_space_constraint(a, pltpu.HBM)
            for a in (
                features[0, 0],
                new_owner[0, 0, :, 0][None],
                rim_rows[0, 0],
                rim_counts[0],
                tile_sources[0, 0].T,
                tile_values[0, 0],
                w_self,
                w_neigh,
                cotangent[0, 0],
            )
        )
    )
    out, g_self, g_neigh = pl.pallas_call(
        finish,
        out_shape=(
            pltpu.HBM((n_rows, hid), BF16),
            pltpu.HBM((width, hid), F32),
            pltpu.HBM((width, hid), F32),
        ),
        in_specs=[any_spec, pl.BlockSpec(memory_space=pltpu.VMEM)],
        out_specs=[any_spec] * 3,
        scratch_shapes=[pltpu.VMEM((2, width, hid), F32), pltpu.SemaphoreType.DMA((3,))],
        compiler_params=pltpu.CompilerParams(vmem_limit_bytes=VMEM_LIMIT),
    )(out, gath)
    return (out[None, None], g_self, g_neigh)


def solution(mesh):
    return jax.shard_map(
        on_device,
        mesh=mesh,
        in_specs=(
            P("group", "dom", None, None),
            P("group", "dom", None, None),
            P("group", "dom", None, None),
            P("group", "dom", None),
            P("group", "dom", None, None),
            P("group", "dom", None, None, None, None),
            P(),
            P(),
            P("group", "dom", None, None),
        ),
        out_specs=(P("group", "dom", None, None), P(), P()),
        check_vma=False,
    )
```

```python
import functools
import math

import jax
import jax.numpy as jnp
from jax import lax
from jax.experimental import pallas as pl
from jax.experimental.pallas import tpu as pltpu
from jax.sharding import PartitionSpec as P

F32 = jnp.float32
BF16 = jnp.bfloat16
I32 = jnp.int32
SIDE = 8
TILE = 128
RB = 8
PIECES = SIDE * SIDE // 2
Z_STEPS = (4, 3, 5, 2, 6, 1, 7)
VMEM_LIMIT = 48 * 1024 * 1024


def ring(d):
    return min(d, SIDE - d)


STEPS = sorted(
    ((dx, dy) for dy in range(SIDE) for dx in range(SIDE) if dx or dy),
    key=lambda s: -ring(s[0]) - ring(s[1]),
)
EVEN = [s for s in STEPS if sum(s) % 2 == 0] + [(0, 0)]
ODD = [s for s in STEPS if sum(s) % 2 == 1]


def iota(shape, axis):
    return lax.broadcasted_iota(I32, shape, axis)


def to_column(row, n):
    grid = jnp.where(iota((n, n), 0) == iota((n, n), 1), jnp.broadcast_to(row, (n, n)), 0)
    return jnp.sum(grid, axis=1, keepdims=True)


def kernel(
    scale,
    feat_hbm,
    owner_hbm,
    rim_hbm,
    cnt_hbm,
    src_hbm,
    val_hbm,
    ws_hbm,
    wn_hbm,
    cot_hbm,
    out_any,
    gath,
    feat,
    owner,
    rim,
    cnt,
    src,
    val,
    ws,
    wn,
    cot,
    out,
    outbox,
    ext,
    pick,
    rim_out,
    x_t,
    pre_self,
    neighbours,
    dpre,
    g_out,
    g_in,
    g_own,
    part,
    recv,
    z_part,
    recv_z,
    total,
    in_sems,
    out_sem,
    a2a_send,
    a2a_recv,
    rim_send,
    rim_recv,
    pair_send,
    pair_recv,
    ph_send,
    ph_recv,
):
    dom = lax.axis_index("dom")
    group = lax.axis_index("group")
    my_x, my_y = lax.rem(dom, SIDE), lax.div(dom, SIDE)
    my_z, core = lax.div(group, 2), lax.rem(group, 2)
    peers = SIDE * SIDE
    n_group = 2 * SIDE
    other = group + 1 - 2 * core

    barrier = pltpu.get_barrier_semaphore()
    group_next = lax.rem(group + 1, n_group)
    group_prev = lax.rem(group + n_group - 1, n_group)
    along_z = [lax.rem(my_z + i, SIDE) * 2 + core for i in Z_STEPS]
    for g in [*along_z, group_next, group_prev]:
        pl.semaphore_signal(barrier, inc=1, device_id={"dom": dom, "group": g})
    in_plane = []
    for dx, dy in STEPS:
        xi, yi = lax.rem(my_x + dx, SIDE), lax.rem(my_y + dy, SIDE)
        in_plane.append((xi, yi, {"dom": yi * SIDE + xi, "group": group}))
        pl.semaphore_signal(barrier, inc=1, device_id=in_plane[-1][2])

    pending = []

    def wait_for(like, sem):
        pltpu.make_async_copy(like, like, sem).wait()

    loads = []
    for k, (a, b) in enumerate(
        (
            (owner_hbm, owner),
            (feat_hbm, feat),
            (rim_hbm, rim),
            (cnt_hbm, cnt),
            (src_hbm, src),
            (ws_hbm, ws),
            (wn_hbm, wn),
            (val_hbm, val),
            (cot_hbm, cot),
        )
    ):
        loads.append(pltpu.make_async_copy(a, b, in_sems.at[k]))
        loads[-1].start()
    l_owner, l_feat, l_rim, l_cnt, l_src, l_ws, l_wn, l_val, l_cot = loads

    blocks = owner.shape[1]
    rows = feat.shape[0]
    l_owner.wait()
    owner_col = to_column(owner[...], blocks)
    block_of = lax.div(iota((blocks, rows), 1), RB)
    block_id = iota((blocks, rows), 0)
    owner_b = jnp.broadcast_to(owner_col, (blocks, rows))
    owner_row = jnp.sum(jnp.where(block_id == block_of, owner_b, 0), axis=0, keepdims=True)
    before = (owner_b == jnp.broadcast_to(owner_row, (blocks, rows))) & (block_id < block_of)
    rank = jnp.sum(jnp.where(before, 1, 0), axis=0, keepdims=True)
    slot_row = (owner_row * 2 + rank) * RB + lax.rem(iota((1, rows), 1), RB)

    l_feat.wait()
    share = 2 * RB
    for j in range(SIDE):
        hot = jnp.where(
            iota((TILE, rows), 0) + j * TILE == jnp.broadcast_to(slot_row, (TILE, rows)),
            1.0,
            0.0,
        ).astype(BF16)
        outbox[j] = jnp.dot(hot, feat[...], preferred_element_type=F32).astype(BF16)
    pl.semaphore_wait(barrier, peers - 1 + SIDE - 1 + 2)
    for xi, yi, target in in_plane:
        pltpu.make_async_remote_copy(
            src_ref=outbox.at[yi, pl.ds(xi * share, share)],
            dst_ref=ext.at[my_y, pl.ds(my_x * share, share)],
            send_sem=a2a_send,
            recv_sem=a2a_recv,
            device_id=target,
        ).start()
    pltpu.make_async_copy(
        outbox.at[my_y, pl.ds(my_x * share, share)],
        ext.at[my_y, pl.ds(my_x * share, share)],
        a2a_recv,
    ).start()
    pending.append(lambda: wait_for(outbox.at[pl.ds(0, SIDE - 1)], a2a_send))
    pending.append(lambda: wait_for(outbox.at[0, pl.ds(0, (SIDE - 1) * share)], a2a_send))

    l_rim.wait()
    l_cnt.wait()
    n_rows = SIDE * TILE
    for p in range(4):
        column = to_column(rim[p : p + 1, :], TILE)
        column = jnp.where(iota((TILE, 1), 0) < cnt[0, p], column, -1)
        pick[p] = jnp.where(
            iota((TILE, n_rows), 1) == jnp.broadcast_to(column, (TILE, n_rows)), 1.0, 0.0
        ).astype(BF16)
    l_ws.wait()
    l_wn.wait()
    l_src.wait()
    l_val.wait()
    l_cot.wait()

    wait_for(ext.at[pl.ds(0, SIDE)], a2a_recv)

    rims = (
        (0, {"dom": lax.rem(dom + 1, peers), "group": group}),
        (1, {"dom": lax.rem(dom + peers - 1, peers), "group": group}),
        (2, {"dom": dom, "group": group_next}),
        (3, {"dom": dom, "group": group_prev}),
    )
    owned = ext[0:SIDE].reshape(n_rows, feat.shape[1])
    rim_copies = []
    for p, target in rims:
        rim_out[p] = jnp.dot(pick[p], owned, preferred_element_type=F32).astype(BF16)
        rim_copies.append(
            pltpu.make_async_remote_copy(
                src_ref=rim_out.at[p],
                dst_ref=ext.at[SIDE + p],
                send_sem=rim_send.at[p],
                recv_sem=rim_recv.at[p],
                device_id=target,
            )
        )
        rim_copies[-1].start()
        pending.append(rim_copies[-1].wait_send)
    for i in range(SIDE):
        x_t[0, :, i * TILE : (i + 1) * TILE] = ext[i].T
    quarter = n_rows // 4
    for h in range(4):
        r = pl.ds(h * quarter, quarter)
        pre_self[r, :] = jnp.dot(
            owned[h * quarter : (h + 1) * quarter], ws[...], preferred_element_type=F32
        )
    for copy in rim_copies:
        copy.wait_recv()

    stores = []
    for i in range(SIDE):
        lhs = jnp.concatenate([val[i, t] for t in range(4)], axis=1)
        rhs = jnp.concatenate([ext[src[t, i]] for t in range(4)], axis=0)
        neighbours[pl.ds(i * TILE, TILE), :] = jnp.dot(
            lhs, rhs, preferred_element_type=F32
        ).astype(BF16)
    for h in range(4):
        r = pl.ds(h * quarter, quarter)
        neigh = neighbours[r, :]
        x_t[1, :, h * quarter : (h + 1) * quarter] = neigh.T
        pre = pre_self[r, :] + jnp.dot(neigh, wn[...], preferred_element_type=F32)
        sig = 0.5 * jnp.tanh(0.5 * pre) + 0.5
        silu = pre * sig
        out[r, :] = silu.astype(BF16)
        dpre[r, :] = (cot[r, :].astype(F32) * (sig + silu * (1.0 - sig))).astype(BF16)

    width = feat.shape[1]
    half = width // 2
    pairs = []
    for h in range(2):
        r = pl.ds(h * half, half)
        g_out[r, :] = jnp.dot(x_t[1 - core, r, :], dpre[...], preferred_element_type=F32)
        pairs.append(
            pltpu.make_async_remote_copy(
                src_ref=g_out.at[r],
                dst_ref=g_in.at[r],
                send_sem=pair_send.at[h],
                recv_sem=pair_recv.at[h],
                device_id={"dom": dom, "group": other},
            )
        )
        pairs[-1].start()
        pending.append(pairs[-1].wait_send)
    g_own[...] = jnp.dot(x_t[core], dpre[...], preferred_element_type=F32)
    for h in range(2):
        pairs[h].wait_recv()
        r = pl.ds(h * half, half)
        summed = g_own[r, :] + g_in[r, :]
        for k in range(PIECES // 2):
            r, c = k // 2 * 16, k % 2 * TILE
            part[h * PIECES // 2 + k] = summed[r : r + 16, c : c + TILE].astype(BF16)

    odd = lax.rem(my_x + my_y + core, 2)
    mine = my_y * (SIDE // 2) + lax.div(my_x, 2)

    def to_owner(dx, dy):
        xi, yi = lax.rem(my_x + dx, SIDE), lax.rem(my_y + dy, SIDE)
        return pltpu.make_async_remote_copy(
            src_ref=part.at[yi * (SIDE // 2) + lax.div(xi, 2)],
            dst_ref=recv.at[dom],
            send_sem=ph_send.at[1],
            recv_sem=ph_recv.at[1],
            device_id={"dom": yi * SIDE + xi, "group": group},
        )

    for (ex, ey), (ox, oy) in zip(EVEN[:-1], ODD[:-1]):
        to_owner(ex + odd * (ox - ex), ey + odd * (oy - ey)).start()

    @pl.when(odd == 1)
    def _():
        to_owner(*ODD[-1]).start()

    store = pltpu.make_async_copy(out, out_any, out_sem)
    store.start()
    pending.append(store.wait)

    @pl.when(odd == 0)
    def _():
        pltpu.make_async_copy(part.at[mine], recv.at[dom], ph_recv.at[1]).start()
        wait_for(recv, ph_recv.at[1])
        z_part[...] = jnp.sum(recv[...].astype(F32), axis=0)

        for g in along_z:
            pltpu.make_async_remote_copy(
                src_ref=z_part,
                dst_ref=recv_z.at[my_z],
                send_sem=ph_send.at[2],
                recv_sem=ph_recv.at[2],
                device_id={"dom": dom, "group": g},
            ).start()
        pltpu.make_async_copy(z_part, recv_z.at[my_z], ph_recv.at[2]).start()
        wait_for(recv_z, ph_recv.at[2])
        total[...] = (jnp.sum(recv_z[...], axis=0) * scale).astype(BF16)

        for _, _, target in in_plane:
            pltpu.make_async_remote_copy(
                src_ref=total,
                dst_ref=gath.at[core, mine],
                send_sem=ph_send.at[3],
                recv_sem=ph_recv.at[3],
                device_id=target,
            ).start()
        pltpu.make_async_copy(total, gath.at[core, mine], ph_recv.at[3]).start()

    wait_for(gath.at[core], ph_recv.at[3])
    back = pltpu.make_async_remote_copy(
        src_ref=gath.at[core],
        dst_ref=gath.at[core],
        send_sem=ph_send.at[4],
        recv_sem=ph_recv.at[4],
        device_id={"dom": dom, "group": other},
    )
    back.start()

    @pl.when(odd == 1)
    def _():
        wait_for(recv.at[pl.ds(0, PIECES)], ph_send.at[1])

    @pl.when(odd == 0)
    def _():
        wait_for(recv.at[pl.ds(0, PIECES - 1)], ph_send.at[1])
        wait_for(recv_z.at[pl.ds(0, SIDE - 1)], ph_send.at[2])
        wait_for(recv.at[pl.ds(0, peers - 1)], ph_send.at[3])

    for wait in pending:
        wait()
    back.wait()


def finish(out_in, gath, out, g_self, g_neigh, grads, sems):
    copies = [pltpu.make_async_copy(out_in, out, sems.at[2])]
    copies[0].start()
    for w, target in enumerate((g_self, g_neigh)):
        for k in range(PIECES):
            r, c = k // 2 * 16, k % 2 * TILE
            grads[w, r : r + 16, c : c + TILE] = gath[w, k].astype(F32)
        copies.append(pltpu.make_async_copy(grads.at[w], target, sems.at[w]))
        copies[-1].start()
    for copy in copies:
        copy.wait()


def on_device(
    features, new_owner, rim_rows, rim_counts, tile_sources, tile_values, w_self, w_neigh, cotangent
):
    rows, width = features.shape[2:]
    blocks = new_owner.shape[2]
    n_rows = cotangent.shape[2]
    hid = w_self.shape[1]
    nodes = rows * lax.axis_size("dom") * lax.axis_size("group")
    scale = 1.0 / math.sqrt(nodes)
    any_spec = pl.BlockSpec(memory_space=pl.ANY)
    out, gath = pl.pallas_call(
        functools.partial(kernel, scale),
        out_shape=(
            pltpu.VMEM((n_rows, hid), BF16),
            pltpu.VMEM((2, PIECES, 16, TILE), BF16),
        ),
        in_specs=[any_spec] * 9,
        out_specs=[any_spec] * 2,
        scratch_shapes=[
            pltpu.VMEM((rows, width), BF16),
            pltpu.VMEM((1, blocks), I32),
            pltpu.VMEM((4, TILE), I32),
            pltpu.SMEM((1, 4), I32),
            pltpu.SMEM((4, SIDE), I32),
            pltpu.VMEM((SIDE, 4, TILE, TILE), BF16),
            pltpu.VMEM((width, hid), BF16),
            pltpu.VMEM((width, hid), BF16),
            pltpu.VMEM((n_rows, hid), BF16),
            pltpu.VMEM((n_rows, hid), BF16),
            pltpu.VMEM((SIDE, TILE, width), BF16),
            pltpu.VMEM((SIDE + 4, TILE, width), BF16),
            pltpu.VMEM((4, TILE, n_rows), BF16),
            pltpu.VMEM((4, TILE, width), BF16),
            pltpu.VMEM((2, width, n_rows), BF16),
            pltpu.VMEM((n_rows, hid), F32),
            pltpu.VMEM((n_rows, width), BF16),
            pltpu.VMEM((n_rows, hid), BF16),
            pltpu.VMEM((width, hid), F32),
            pltpu.VMEM((width, hid), F32),
            pltpu.VMEM((width, hid), F32),
            pltpu.VMEM((PIECES, 16, TILE), BF16),
            pltpu.VMEM((SIDE * SIDE, 16, TILE), BF16),
            pltpu.VMEM((16, TILE), F32),
            pltpu.VMEM((SIDE, 16, TILE), F32),
            pltpu.VMEM((16, TILE), BF16),
            pltpu.SemaphoreType.DMA((9,)),
            pltpu.SemaphoreType.DMA,
            pltpu.SemaphoreType.DMA,
            pltpu.SemaphoreType.DMA,
            pltpu.SemaphoreType.DMA((4,)),
            pltpu.SemaphoreType.DMA((4,)),
            pltpu.SemaphoreType.DMA((2,)),
            pltpu.SemaphoreType.DMA((2,)),
            pltpu.SemaphoreType.DMA((5,)),
            pltpu.SemaphoreType.DMA((5,)),
        ],
        compiler_params=pltpu.CompilerParams(
            collective_id=0, has_side_effects=True, vmem_limit_bytes=VMEM_LIMIT
        ),
    )(
        *(
            pltpu.with_memory_space_constraint(a, pltpu.HBM)
            for a in (
                features[0, 0],
                new_owner[0, 0, :, 0][None],
                rim_rows[0, 0],
                rim_counts[0],
                tile_sources[0, 0].T,
                tile_values[0, 0],
                w_self,
                w_neigh,
                cotangent[0, 0],
            )
        )
    )
    out, g_self, g_neigh = pl.pallas_call(
        finish,
        out_shape=(
            pltpu.HBM((n_rows, hid), BF16),
            pltpu.HBM((width, hid), F32),
            pltpu.HBM((width, hid), F32),
        ),
        in_specs=[any_spec, pl.BlockSpec(memory_space=pltpu.VMEM)],
        out_specs=[any_spec] * 3,
        scratch_shapes=[pltpu.VMEM((2, width, hid), F32), pltpu.SemaphoreType.DMA((3,))],
        compiler_params=pltpu.CompilerParams(vmem_limit_bytes=VMEM_LIMIT),
    )(out, gath)
    return (out[None, None], g_self, g_neigh)


def solution(mesh):
    return jax.shard_map(
        on_device,
        mesh=mesh,
        in_specs=(
            P("group", "dom", None, None),
            P("group", "dom", None, None),
            P("group", "dom", None, None),
            P("group", "dom", None),
            P("group", "dom", None, None),
            P("group", "dom", None, None, None, None),
            P(),
            P(),
            P("group", "dom", None, None),
        ),
        out_specs=(P("group", "dom", None, None), P(), P()),
        check_vma=False,
    )
```

```python
import functools
import math

import jax
import jax.numpy as jnp
from jax import lax
from jax.experimental import pallas as pl
from jax.experimental.pallas import tpu as pltpu
from jax.sharding import PartitionSpec as P

F32 = jnp.float32
BF16 = jnp.bfloat16
I32 = jnp.int32
SIDE = 8
TILE = 128
RB = 8
PIECES = SIDE * SIDE // 2
FAR_PIECE = SIDE // 2 * (SIDE // 2) + SIDE // 4
Z_STEPS = (4, 3, 5, 2, 6, 1, 7)
VMEM_LIMIT = 48 * 1024 * 1024


def ring(d):
    return min(d, SIDE - d)


STEPS = sorted(
    ((dx, dy) for dy in range(SIDE) for dx in range(SIDE) if dx or dy),
    key=lambda s: -ring(s[0]) - ring(s[1]),
)
EVEN = [s for s in STEPS if sum(s) % 2 == 0] + [(0, 0)]
ODD = [s for s in STEPS if sum(s) % 2 == 1]


def homeward(fx, fy):
    xs, ys = ([3, 4, 5, 6] if f else [7, 0, 1, 2] for f in (fx, fy))

    def left(step):
        return sum(ring((x + step[0]) % SIDE) for x in xs) + sum(
            ring((y + step[1]) % SIDE) for y in ys
        )

    return sorted(STEPS, key=left)


HOMEWARD = {(fx, fy): homeward(fx, fy) for fx in (0, 1) for fy in (0, 1)}


def farthest(x, y):
    return 1 - lax.div((x - 4) * (x - 4) + (y - 4) * (y - 4) + 31, 32)


def iota(shape, axis):
    return lax.broadcasted_iota(I32, shape, axis)


def to_column(row, n):
    grid = jnp.where(iota((n, n), 0) == iota((n, n), 1), jnp.broadcast_to(row, (n, n)), 0)
    return jnp.sum(grid, axis=1, keepdims=True)


def kernel(
    scale,
    feat_hbm,
    owner_hbm,
    rim_hbm,
    cnt_hbm,
    src_hbm,
    val_hbm,
    ws_hbm,
    wn_hbm,
    cot_hbm,
    out_any,
    gath,
    feat,
    owner,
    rim,
    cnt,
    src,
    val,
    ws,
    wn,
    cot,
    out,
    outbox,
    ext,
    pick,
    rim_out,
    x_t,
    pre_self,
    neighbours,
    dpre,
    g_out,
    g_in,
    g_own,
    part,
    recv,
    z_part,
    recv_z,
    total,
    in_sems,
    out_sem,
    a2a_send,
    a2a_recv,
    rim_send,
    rim_recv,
    pair_send,
    pair_recv,
    ph_send,
    ph_recv,
):
    dom = lax.axis_index("dom")
    group = lax.axis_index("group")
    my_x, my_y = lax.rem(dom, SIDE), lax.div(dom, SIDE)
    my_z, core = lax.div(group, 2), lax.rem(group, 2)
    peers = SIDE * SIDE
    n_group = 2 * SIDE
    other = group + 1 - 2 * core

    pairs_in = (
        (owner_hbm, owner),
        (feat_hbm, feat),
        (rim_hbm, rim),
        (cnt_hbm, cnt),
        (src_hbm, src),
        (ws_hbm, ws),
        (wn_hbm, wn),
        (val_hbm, val),
        (cot_hbm, cot),
    )
    loads = [
        pltpu.make_async_copy(a, b, in_sems.at[k]) for k, (a, b) in enumerate(pairs_in)
    ]
    l_owner, l_feat, l_rim, l_cnt, l_src, l_ws, l_wn, l_val, l_cot = loads
    l_owner.start()
    l_feat.start()

    barrier = pltpu.get_barrier_semaphore()
    group_next = lax.rem(group + 1, n_group)
    group_prev = lax.rem(group + n_group - 1, n_group)
    along_z = [lax.rem(my_z + i, SIDE) * 2 + core for i in Z_STEPS]
    for g in [*along_z, group_next, group_prev]:
        pl.semaphore_signal(barrier, inc=1, device_id={"dom": dom, "group": g})
    in_plane = []
    for dx, dy in STEPS:
        xi, yi = lax.rem(my_x + dx, SIDE), lax.rem(my_y + dy, SIDE)
        in_plane.append((xi, yi, {"dom": yi * SIDE + xi, "group": group}))
        pl.semaphore_signal(barrier, inc=1, device_id=in_plane[-1][2])

    for load in loads[2:]:
        load.start()

    pending = []

    def wait_for(like, sem):
        pltpu.make_async_copy(like, like, sem).wait()


    blocks = owner.shape[1]
    rows = feat.shape[0]
    l_owner.wait()
    owner_col = to_column(owner[...], blocks)
    block_of = lax.div(iota((blocks, rows), 1), RB)
    block_id = iota((blocks, rows), 0)
    owner_b = jnp.broadcast_to(owner_col, (blocks, rows))
    owner_row = jnp.sum(jnp.where(block_id == block_of, owner_b, 0), axis=0, keepdims=True)
    before = (owner_b == jnp.broadcast_to(owner_row, (blocks, rows))) & (block_id < block_of)
    rank = jnp.sum(jnp.where(before, 1, 0), axis=0, keepdims=True)
    slot_row = (owner_row * 2 + rank) * RB + lax.rem(iota((1, rows), 1), RB)

    l_feat.wait()
    share = 2 * RB
    for j in range(SIDE):
        hot = jnp.where(
            iota((TILE, rows), 0) + j * TILE == jnp.broadcast_to(slot_row, (TILE, rows)),
            1.0,
            0.0,
        ).astype(BF16)
        outbox[j] = jnp.dot(hot, feat[...], preferred_element_type=F32).astype(BF16)
    pl.semaphore_wait(barrier, peers - 1 + SIDE - 1 + 2)
    for xi, yi, target in in_plane:
        pltpu.make_async_remote_copy(
            src_ref=outbox.at[yi, pl.ds(xi * share, share)],
            dst_ref=ext.at[my_y, pl.ds(my_x * share, share)],
            send_sem=a2a_send,
            recv_sem=a2a_recv,
            device_id=target,
        ).start()
    pltpu.make_async_copy(
        outbox.at[my_y, pl.ds(my_x * share, share)],
        ext.at[my_y, pl.ds(my_x * share, share)],
        a2a_recv,
    ).start()
    pending.append(lambda: wait_for(outbox.at[pl.ds(0, SIDE - 1)], a2a_send))
    pending.append(lambda: wait_for(outbox.at[0, pl.ds(0, (SIDE - 1) * share)], a2a_send))

    l_rim.wait()
    l_cnt.wait()
    n_rows = SIDE * TILE
    for p in range(4):
        column = to_column(rim[p : p + 1, :], TILE)
        column = jnp.where(iota((TILE, 1), 0) < cnt[0, p], column, -1)
        pick[p] = jnp.where(
            iota((TILE, n_rows), 1) == jnp.broadcast_to(column, (TILE, n_rows)), 1.0, 0.0
        ).astype(BF16)
    l_ws.wait()
    l_wn.wait()
    l_src.wait()
    l_val.wait()
    l_cot.wait()

    wait_for(ext.at[pl.ds(0, SIDE)], a2a_recv)

    rims = (
        (0, {"dom": lax.rem(dom + 1, peers), "group": group}),
        (1, {"dom": lax.rem(dom + peers - 1, peers), "group": group}),
        (2, {"dom": dom, "group": group_next}),
        (3, {"dom": dom, "group": group_prev}),
    )
    owned = ext[0:SIDE].reshape(n_rows, feat.shape[1])
    rim_copies = []
    for p, target in rims:
        rim_out[p] = jnp.dot(pick[p], owned, preferred_element_type=F32).astype(BF16)
        rim_copies.append(
            pltpu.make_async_remote_copy(
                src_ref=rim_out.at[p],
                dst_ref=ext.at[SIDE + p],
                send_sem=rim_send.at[p],
                recv_sem=rim_recv.at[p],
                device_id=target,
            )
        )
        rim_copies[-1].start()
        pending.append(rim_copies[-1].wait_send)
    for i in range(SIDE):
        x_t[0, :, i * TILE : (i + 1) * TILE] = ext[i].T
    quarter = n_rows // 4
    for h in range(4):
        r = pl.ds(h * quarter, quarter)
        pre_self[r, :] = jnp.dot(
            owned[h * quarter : (h + 1) * quarter], ws[...], preferred_element_type=F32
        )
    for copy in rim_copies:
        copy.wait_recv()

    stores = []
    for i in range(SIDE):
        lhs = jnp.concatenate([val[i, t] for t in range(4)], axis=1)
        rhs = jnp.concatenate([ext[src[t, i]] for t in range(4)], axis=0)
        neighbours[pl.ds(i * TILE, TILE), :] = jnp.dot(
            lhs, rhs, preferred_element_type=F32
        ).astype(BF16)
    for h in range(4):
        r = pl.ds(h * quarter, quarter)
        neigh = neighbours[r, :]
        x_t[1, :, h * quarter : (h + 1) * quarter] = neigh.T
        pre = pre_self[r, :] + jnp.dot(neigh, wn[...], preferred_element_type=F32)
        sig = 0.5 * jnp.tanh(0.5 * pre) + 0.5
        silu = pre * sig
        out[r, :] = silu.astype(BF16)
        dpre[r, :] = (cot[r, :].astype(F32) * (sig + silu * (1.0 - sig))).astype(BF16)

    width = feat.shape[1]
    half = width // 2
    pairs = []
    for h in range(2):
        r = pl.ds(h * half, half)
        g_out[r, :] = jnp.dot(x_t[1 - core, r, :], dpre[...], preferred_element_type=F32)
        pairs.append(
            pltpu.make_async_remote_copy(
                src_ref=g_out.at[r],
                dst_ref=g_in.at[r],
                send_sem=pair_send.at[h],
                recv_sem=pair_recv.at[h],
                device_id={"dom": dom, "group": other},
            )
        )
        pairs[-1].start()
        pending.append(pairs[-1].wait_send)
    g_own[...] = jnp.dot(x_t[core], dpre[...], preferred_element_type=F32)
    for h in range(2):
        pairs[h].wait_recv()
        r = pl.ds(h * half, half)
        summed = g_own[r, :] + g_in[r, :]
        for k in range(PIECES // 2):
            r, c = k // 2 * 16, k % 2 * TILE
            part[h * PIECES // 2 + k] = summed[r : r + 16, c : c + TILE].astype(BF16)

    odd = lax.rem(my_x + my_y + core, 2)
    far = farthest(my_x, my_y) * (1 - core)
    stand_in = 1 - lax.div((my_x - 1) * (my_x - 1) + my_y * my_y + core + 127, 128)
    owns = (1 - odd) * (1 - far) + stand_in
    mine = my_y * (SIDE // 2) + lax.div(my_x, 2) + stand_in * FAR_PIECE

    def to_owner(dx, dy):
        xi, yi = lax.rem(my_x + dx, SIDE), lax.rem(my_y + dy, SIDE)
        moved = farthest(xi, yi) * (1 - core)
        return pltpu.make_async_remote_copy(
            src_ref=part.at[yi * (SIDE // 2) + lax.div(xi, 2)],
            dst_ref=recv.at[dom],
            send_sem=ph_send.at[1],
            recv_sem=ph_recv.at[1],
            device_id={
                "dom": (yi - 4 * moved) * SIDE + xi - 3 * moved,
                "group": group,
            },
        )

    for (ex, ey), (ox, oy) in zip(EVEN[:-1], ODD[:-1]):
        copy = to_owner(ex + odd * (ox - ex), ey + odd * (oy - ey))
        if (ox, oy) == (3, 4):
            pl.when(stand_in == 0)(copy.start)
        else:
            copy.start()

    @pl.when(far == 1)
    def _():
        to_owner(0, 0).start()

    @pl.when(odd == 1)
    def _():
        to_owner(*ODD[-1]).start()

    store = pltpu.make_async_copy(out, out_any, out_sem)
    store.start()
    pending.append(store.wait)

    @pl.when(owns == 1)
    def _():
        pltpu.make_async_copy(part.at[mine], recv.at[dom], ph_recv.at[1]).start()
        wait_for(recv, ph_recv.at[1])
        z_part[...] = jnp.sum(recv[...].astype(F32), axis=0)

        for g in along_z:
            pltpu.make_async_remote_copy(
                src_ref=z_part,
                dst_ref=recv_z.at[my_z],
                send_sem=ph_send.at[2],
                recv_sem=ph_recv.at[2],
                device_id={"dom": dom, "group": g},
            ).start()
        pltpu.make_async_copy(z_part, recv_z.at[my_z], ph_recv.at[2]).start()
        wait_for(recv_z, ph_recv.at[2])
        total[...] = (jnp.sum(recv_z[...], axis=0) * scale).astype(BF16)

        far_x = 1 - lax.div(lax.rem(my_x + 5, SIDE), 4)
        far_y = 1 - lax.div(lax.rem(my_y + 5, SIDE), 4)

        def to_plane(steps):
            for dx, dy in steps:
                xi, yi = lax.rem(my_x + dx, SIDE), lax.rem(my_y + dy, SIDE)
                pltpu.make_async_remote_copy(
                    src_ref=total,
                    dst_ref=gath.at[core, mine],
                    send_sem=ph_send.at[3],
                    recv_sem=ph_recv.at[3],
                    device_id={"dom": yi * SIDE + xi, "group": group},
                ).start()

        for (fx, fy), steps in HOMEWARD.items():
            pl.when((far_x * 2 + far_y) == fx * 2 + fy)(functools.partial(to_plane, steps))
        pltpu.make_async_copy(total, gath.at[core, mine], ph_recv.at[3]).start()

    wait_for(gath.at[core], ph_recv.at[3])
    back = pltpu.make_async_remote_copy(
        src_ref=gath.at[core],
        dst_ref=gath.at[core],
        send_sem=ph_send.at[4],
        recv_sem=ph_recv.at[4],
        device_id={"dom": dom, "group": other},
    )
    back.start()

    @pl.when(owns == 0)
    def _():
        wait_for(recv.at[pl.ds(0, PIECES)], ph_send.at[1])

    @pl.when(owns == 1)
    def _():
        wait_for(recv.at[pl.ds(0, PIECES - 1)], ph_send.at[1])
        wait_for(recv_z.at[pl.ds(0, SIDE - 1)], ph_send.at[2])
        wait_for(recv.at[pl.ds(0, peers - 1)], ph_send.at[3])

    for wait in pending:
        wait()
    back.wait()


def finish(out_in, gath, out, g_self, g_neigh, grads, sems):
    copies = [pltpu.make_async_copy(out_in, out, sems.at[2])]
    copies[0].start()
    for w, target in enumerate((g_self, g_neigh)):
        for k in range(PIECES):
            r, c = k // 2 * 16, k % 2 * TILE
            grads[w, r : r + 16, c : c + TILE] = gath[w, k].astype(F32)
        copies.append(pltpu.make_async_copy(grads.at[w], target, sems.at[w]))
        copies[-1].start()
    for copy in copies:
        copy.wait()


def on_device(
    features, new_owner, rim_rows, rim_counts, tile_sources, tile_values, w_self, w_neigh, cotangent
):
    rows, width = features.shape[2:]
    blocks = new_owner.shape[2]
    n_rows = cotangent.shape[2]
    hid = w_self.shape[1]
    nodes = rows * lax.axis_size("dom") * lax.axis_size("group")
    scale = 1.0 / math.sqrt(nodes)
    any_spec = pl.BlockSpec(memory_space=pl.ANY)
    out, gath = pl.pallas_call(
        functools.partial(kernel, scale),
        out_shape=(
            pltpu.VMEM((n_rows, hid), BF16),
            pltpu.VMEM((2, PIECES, 16, TILE), BF16),
        ),
        in_specs=[any_spec] * 9,
        out_specs=[any_spec] * 2,
        scratch_shapes=[
            pltpu.VMEM((rows, width), BF16),
            pltpu.VMEM((1, blocks), I32),
            pltpu.VMEM((4, TILE), I32),
            pltpu.SMEM((1, 4), I32),
            pltpu.SMEM((4, SIDE), I32),
            pltpu.VMEM((SIDE, 4, TILE, TILE), BF16),
            pltpu.VMEM((width, hid), BF16),
            pltpu.VMEM((width, hid), BF16),
            pltpu.VMEM((n_rows, hid), BF16),
            pltpu.VMEM((n_rows, hid), BF16),
            pltpu.VMEM((SIDE, TILE, width), BF16),
            pltpu.VMEM((SIDE + 4, TILE, width), BF16),
            pltpu.VMEM((4, TILE, n_rows), BF16),
            pltpu.VMEM((4, TILE, width), BF16),
            pltpu.VMEM((2, width, n_rows), BF16),
            pltpu.VMEM((n_rows, hid), F32),
            pltpu.VMEM((n_rows, width), BF16),
            pltpu.VMEM((n_rows, hid), BF16),
            pltpu.VMEM((width, hid), F32),
            pltpu.VMEM((width, hid), F32),
            pltpu.VMEM((width, hid), F32),
            pltpu.VMEM((PIECES, 16, TILE), BF16),
            pltpu.VMEM((SIDE * SIDE, 16, TILE), BF16),
            pltpu.VMEM((16, TILE), F32),
            pltpu.VMEM((SIDE, 16, TILE), F32),
            pltpu.VMEM((16, TILE), BF16),
            pltpu.SemaphoreType.DMA((9,)),
            pltpu.SemaphoreType.DMA,
            pltpu.SemaphoreType.DMA,
            pltpu.SemaphoreType.DMA,
            pltpu.SemaphoreType.DMA((4,)),
            pltpu.SemaphoreType.DMA((4,)),
            pltpu.SemaphoreType.DMA((2,)),
            pltpu.SemaphoreType.DMA((2,)),
            pltpu.SemaphoreType.DMA((5,)),
            pltpu.SemaphoreType.DMA((5,)),
        ],
        compiler_params=pltpu.CompilerParams(
            collective_id=0, has_side_effects=True, vmem_limit_bytes=VMEM_LIMIT
        ),
    )(
        *(
            pltpu.with_memory_space_constraint(a, pltpu.HBM)
            for a in (
                features[0, 0],
                new_owner[0, 0, :, 0][None],
                rim_rows[0, 0],
                rim_counts[0],
                tile_sources[0, 0].T,
                tile_values[0, 0],
                w_self,
                w_neigh,
                cotangent[0, 0],
            )
        )
    )
    out, g_self, g_neigh = pl.pallas_call(
        finish,
        out_shape=(
            pltpu.HBM((n_rows, hid), BF16),
            pltpu.HBM((width, hid), F32),
            pltpu.HBM((width, hid), F32),
        ),
        in_specs=[any_spec, pl.BlockSpec(memory_space=pltpu.VMEM)],
        out_specs=[any_spec] * 3,
        scratch_shapes=[pltpu.VMEM((2, width, hid), F32), pltpu.SemaphoreType.DMA((3,))],
        compiler_params=pltpu.CompilerParams(vmem_limit_bytes=VMEM_LIMIT),
    )(out, gath)
    return (out[None, None], g_self, g_neigh)


def solution(mesh):
    return jax.shard_map(
        on_device,
        mesh=mesh,
        in_specs=(
            P("group", "dom", None, None),
            P("group", "dom", None, None),
            P("group", "dom", None, None),
            P("group", "dom", None),
            P("group", "dom", None, None),
            P("group", "dom", None, None, None, None),
            P(),
            P(),
            P("group", "dom", None, None),
        ),
        out_specs=(P("group", "dom", None, None), P(), P()),
        check_vma=False,
    )
```

```python
import functools
import math

import jax
import jax.numpy as jnp
from jax import lax
from jax.experimental import pallas as pl
from jax.experimental.pallas import tpu as pltpu
from jax.sharding import PartitionSpec as P

F32 = jnp.float32
BF16 = jnp.bfloat16
I32 = jnp.int32
SIDE = 8
TILE = 128
RB = 8
PIECES = SIDE * SIDE // 2
FAR_PIECE = SIDE // 2 * (SIDE // 2) + SIDE // 4
Z_STEPS = (1, 2, 3, 4, 5, 6, 7)
PARTS = 4
VMEM_LIMIT = 48 * 1024 * 1024


def ring(d):
    return min(d, SIDE - d)


STEPS = sorted(
    ((dx, dy) for dy in range(SIDE) for dx in range(SIDE) if dx or dy),
    key=lambda s: -ring(s[0]) - ring(s[1]),
)
EVEN = [s for s in STEPS if sum(s) % 2 == 0] + [(0, 0)]
ODD = [s for s in STEPS if sum(s) % 2 == 1]


def homeward(fx, fy):
    xs, ys = ([3, 4, 5, 6] if f else [7, 0, 1, 2] for f in (fx, fy))

    def left(step):
        return sum(ring((x + step[0]) % SIDE) for x in xs) + sum(
            ring((y + step[1]) % SIDE) for y in ys
        )

    return sorted(STEPS, key=left)


HOMEWARD = {(fx, fy): homeward(fx, fy) for fx in (0, 1) for fy in (0, 1)}


def farthest(x, y):
    return 1 - lax.div((x - 4) * (x - 4) + (y - 4) * (y - 4) + 31, 32)


def iota(shape, axis):
    return lax.broadcasted_iota(I32, shape, axis)


def to_column(row, n):
    grid = jnp.where(iota((n, n), 0) == iota((n, n), 1), jnp.broadcast_to(row, (n, n)), 0)
    return jnp.sum(grid, axis=1, keepdims=True)


def kernel(
    scale,
    feat_hbm,
    owner_hbm,
    rim_hbm,
    cnt_hbm,
    src_hbm,
    val_hbm,
    ws_hbm,
    wn_hbm,
    cot_hbm,
    out_any,
    gath,
    feat,
    owner,
    rim,
    cnt,
    src,
    val,
    ws,
    wn,
    cot,
    out,
    outbox,
    ext,
    pick,
    rim_out,
    x_t,
    pre_self,
    neighbours,
    dpre,
    g_out,
    g_in,
    g_own,
    part,
    recv,
    z_part,
    recv_z,
    total,
    in_sems,
    out_sem,
    a2a_send,
    a2a_recv,
    rim_send,
    rim_recv,
    pair_send,
    pair_recv,
    ph_send,
    ph_recv,
):
    dom = lax.axis_index("dom")
    group = lax.axis_index("group")
    my_x, my_y = lax.rem(dom, SIDE), lax.div(dom, SIDE)
    my_z, core = lax.div(group, 2), lax.rem(group, 2)
    peers = SIDE * SIDE
    n_group = 2 * SIDE
    other = group + 1 - 2 * core

    pairs_in = (
        (owner_hbm, owner),
        (feat_hbm, feat),
        (rim_hbm, rim),
        (cnt_hbm, cnt),
        (src_hbm, src),
        (ws_hbm, ws),
        (wn_hbm, wn),
        (val_hbm, val),
        (cot_hbm, cot),
    )
    loads = [
        pltpu.make_async_copy(a, b, in_sems.at[k]) for k, (a, b) in enumerate(pairs_in)
    ]
    l_owner, l_feat, l_rim, l_cnt, l_src, l_ws, l_wn, l_val, l_cot = loads
    l_owner.start()
    l_feat.start()

    barrier = pltpu.get_barrier_semaphore()
    group_next = lax.rem(group + 1, n_group)
    group_prev = lax.rem(group + n_group - 1, n_group)
    along_z = [lax.rem(my_z + i, SIDE) * 2 + core for i in Z_STEPS]
    for g in [*along_z, group_next, group_prev]:
        pl.semaphore_signal(barrier, inc=1, device_id={"dom": dom, "group": g})
    in_plane = []
    for dx, dy in STEPS:
        xi, yi = lax.rem(my_x + dx, SIDE), lax.rem(my_y + dy, SIDE)
        in_plane.append((xi, yi, {"dom": yi * SIDE + xi, "group": group}))
        pl.semaphore_signal(barrier, inc=1, device_id=in_plane[-1][2])

    for load in loads[2:]:
        load.start()

    pending = []

    def wait_for(like, sem):
        pltpu.make_async_copy(like, like, sem).wait()


    blocks = owner.shape[1]
    rows = feat.shape[0]
    l_owner.wait()
    owner_col = to_column(owner[...], blocks)
    block_of = lax.div(iota((blocks, rows), 1), RB)
    block_id = iota((blocks, rows), 0)
    owner_b = jnp.broadcast_to(owner_col, (blocks, rows))
    owner_row = jnp.sum(jnp.where(block_id == block_of, owner_b, 0), axis=0, keepdims=True)
    before = (owner_b == jnp.broadcast_to(owner_row, (blocks, rows))) & (block_id < block_of)
    rank = jnp.sum(jnp.where(before, 1, 0), axis=0, keepdims=True)
    slot_row = (owner_row * 2 + rank) * RB + lax.rem(iota((1, rows), 1), RB)

    l_feat.wait()
    share = 2 * RB
    for j in range(SIDE):
        hot = jnp.where(
            iota((TILE, rows), 0) + j * TILE == jnp.broadcast_to(slot_row, (TILE, rows)),
            1.0,
            0.0,
        ).astype(BF16)
        outbox[j] = jnp.dot(hot, feat[...], preferred_element_type=F32).astype(BF16)
    pl.semaphore_wait(barrier, peers - 1 + SIDE - 1 + 2)
    for xi, yi, target in in_plane:
        pltpu.make_async_remote_copy(
            src_ref=outbox.at[yi, pl.ds(xi * share, share)],
            dst_ref=ext.at[my_y, pl.ds(my_x * share, share)],
            send_sem=a2a_send,
            recv_sem=a2a_recv,
            device_id=target,
        ).start()
    pltpu.make_async_copy(
        outbox.at[my_y, pl.ds(my_x * share, share)],
        ext.at[my_y, pl.ds(my_x * share, share)],
        a2a_recv,
    ).start()
    pending.append(lambda: wait_for(outbox.at[pl.ds(0, SIDE - 1)], a2a_send))
    pending.append(lambda: wait_for(outbox.at[0, pl.ds(0, (SIDE - 1) * share)], a2a_send))

    l_rim.wait()
    l_cnt.wait()
    n_rows = SIDE * TILE
    for p in range(4):
        column = to_column(rim[p : p + 1, :], TILE)
        column = jnp.where(iota((TILE, 1), 0) < cnt[0, p], column, -1)
        pick[p] = jnp.where(
            iota((TILE, n_rows), 1) == jnp.broadcast_to(column, (TILE, n_rows)), 1.0, 0.0
        ).astype(BF16)
    l_ws.wait()
    l_wn.wait()
    l_src.wait()
    l_val.wait()
    l_cot.wait()

    wait_for(ext.at[pl.ds(0, SIDE)], a2a_recv)

    rims = (
        (0, {"dom": lax.rem(dom + 1, peers), "group": group}),
        (1, {"dom": lax.rem(dom + peers - 1, peers), "group": group}),
        (2, {"dom": dom, "group": group_next}),
        (3, {"dom": dom, "group": group_prev}),
    )
    owned = ext[0:SIDE].reshape(n_rows, feat.shape[1])
    rim_copies = []
    for p, target in rims:
        rim_out[p] = jnp.dot(pick[p], owned, preferred_element_type=F32).astype(BF16)
        rim_copies.append(
            pltpu.make_async_remote_copy(
                src_ref=rim_out.at[p],
                dst_ref=ext.at[SIDE + p],
                send_sem=rim_send.at[p],
                recv_sem=rim_recv.at[p],
                device_id=target,
            )
        )
        rim_copies[-1].start()
        pending.append(rim_copies[-1].wait_send)
    for i in range(SIDE):
        x_t[0, :, i * TILE : (i + 1) * TILE] = ext[i].T
    quarter = n_rows // 4
    for h in range(4):
        r = pl.ds(h * quarter, quarter)
        pre_self[r, :] = jnp.dot(
            owned[h * quarter : (h + 1) * quarter], ws[...], preferred_element_type=F32
        )
    for copy in rim_copies:
        copy.wait_recv()

    stores = []
    for i in range(SIDE):
        lhs = jnp.concatenate([val[i, t] for t in range(4)], axis=1)
        rhs = jnp.concatenate([ext[src[t, i]] for t in range(4)], axis=0)
        neighbours[pl.ds(i * TILE, TILE), :] = jnp.dot(
            lhs, rhs, preferred_element_type=F32
        ).astype(BF16)
    for h in range(4):
        r = pl.ds(h * quarter, quarter)
        neigh = neighbours[r, :]
        x_t[1, :, h * quarter : (h + 1) * quarter] = neigh.T
        pre = pre_self[r, :] + jnp.dot(neigh, wn[...], preferred_element_type=F32)
        sig = 0.5 * jnp.tanh(0.5 * pre) + 0.5
        silu = pre * sig
        out[r, :] = silu.astype(BF16)
        dpre[r, :] = (cot[r, :].astype(F32) * (sig + silu * (1.0 - sig))).astype(BF16)

    width = feat.shape[1]
    chunk = width // PARTS
    pairs = []
    for h in range(PARTS):
        r = pl.ds(h * chunk, chunk)
        g_out[r, :] = jnp.dot(x_t[1 - core, r, :], dpre[...], preferred_element_type=F32)
        pairs.append(
            pltpu.make_async_remote_copy(
                src_ref=g_out.at[r],
                dst_ref=g_in.at[r],
                send_sem=pair_send.at[h],
                recv_sem=pair_recv.at[h],
                device_id={"dom": dom, "group": other},
            )
        )
        pairs[-1].start()
        pending.append(pairs[-1].wait_send)
    g_own[...] = jnp.dot(x_t[core], dpre[...], preferred_element_type=F32)
    for h in range(PARTS):
        pairs[h].wait_recv()
        r = pl.ds(h * chunk, chunk)
        summed = g_own[r, :] + g_in[r, :]
        for k in range(PIECES // PARTS):
            r, c = k // 2 * 16, k % 2 * TILE
            part[h * PIECES // PARTS + k] = summed[r : r + 16, c : c + TILE].astype(BF16)

    odd = lax.rem(my_x + my_y + core, 2)
    far = farthest(my_x, my_y) * (1 - core)
    stand_in = 1 - lax.div((my_x - 1) * (my_x - 1) + my_y * my_y + core + 127, 128)
    owns = (1 - odd) * (1 - far) + stand_in
    mine = my_y * (SIDE // 2) + lax.div(my_x, 2) + stand_in * FAR_PIECE

    def to_owner(dx, dy):
        xi, yi = lax.rem(my_x + dx, SIDE), lax.rem(my_y + dy, SIDE)
        moved = farthest(xi, yi) * (1 - core)
        return pltpu.make_async_remote_copy(
            src_ref=part.at[yi * (SIDE // 2) + lax.div(xi, 2)],
            dst_ref=recv.at[dom],
            send_sem=ph_send.at[1],
            recv_sem=ph_recv.at[1],
            device_id={
                "dom": (yi - 4 * moved) * SIDE + xi - 3 * moved,
                "group": group,
            },
        )

    for (ex, ey), (ox, oy) in zip(EVEN[:-1], ODD[:-1]):
        copy = to_owner(ex + odd * (ox - ex), ey + odd * (oy - ey))
        if (ox, oy) == (3, 4):
            pl.when(stand_in == 0)(copy.start)
        else:
            copy.start()

    @pl.when(far == 1)
    def _():
        to_owner(0, 0).start()

    @pl.when(odd == 1)
    def _():
        to_owner(*ODD[-1]).start()

    store = pltpu.make_async_copy(out, out_any, out_sem)
    store.start()
    pending.append(store.wait)

    @pl.when(owns == 1)
    def _():
        pltpu.make_async_copy(part.at[mine], recv.at[dom], ph_recv.at[1]).start()
        wait_for(recv, ph_recv.at[1])
        z_part[...] = jnp.sum(recv[...].astype(F32), axis=0)

        for g in along_z:
            pltpu.make_async_remote_copy(
                src_ref=z_part,
                dst_ref=recv_z.at[my_z],
                send_sem=ph_send.at[2],
                recv_sem=ph_recv.at[2],
                device_id={"dom": dom, "group": g},
            ).start()
        pltpu.make_async_copy(z_part, recv_z.at[my_z], ph_recv.at[2]).start()
        wait_for(recv_z, ph_recv.at[2])
        total[...] = (jnp.sum(recv_z[...], axis=0) * scale).astype(BF16)

        far_x = 1 - lax.div(lax.rem(my_x + 5, SIDE), 4)
        far_y = 1 - lax.div(lax.rem(my_y + 5, SIDE), 4)

        def to_plane(steps):
            for dx, dy in steps:
                xi, yi = lax.rem(my_x + dx, SIDE), lax.rem(my_y + dy, SIDE)
                pltpu.make_async_remote_copy(
                    src_ref=total,
                    dst_ref=gath.at[core, mine],
                    send_sem=ph_send.at[3],
                    recv_sem=ph_recv.at[3],
                    device_id={"dom": yi * SIDE + xi, "group": group},
                ).start()

        for (fx, fy), steps in HOMEWARD.items():
            pl.when((far_x * 2 + far_y) == fx * 2 + fy)(functools.partial(to_plane, steps))
        pltpu.make_async_copy(total, gath.at[core, mine], ph_recv.at[3]).start()

    wait_for(gath.at[core], ph_recv.at[3])
    back = pltpu.make_async_remote_copy(
        src_ref=gath.at[core],
        dst_ref=gath.at[core],
        send_sem=ph_send.at[4],
        recv_sem=ph_recv.at[4],
        device_id={"dom": dom, "group": other},
    )
    back.start()

    @pl.when(owns == 0)
    def _():
        wait_for(recv.at[pl.ds(0, PIECES)], ph_send.at[1])

    @pl.when(owns == 1)
    def _():
        wait_for(recv.at[pl.ds(0, PIECES - 1)], ph_send.at[1])
        wait_for(recv_z.at[pl.ds(0, SIDE - 1)], ph_send.at[2])
        wait_for(recv.at[pl.ds(0, peers - 1)], ph_send.at[3])

    for wait in pending:
        wait()
    back.wait()


def finish(out_in, gath, out, g_self, g_neigh, grads, sems):
    copies = [pltpu.make_async_copy(out_in, out, sems.at[2])]
    copies[0].start()
    for w, target in enumerate((g_self, g_neigh)):
        for k in range(PIECES):
            r, c = k // 2 * 16, k % 2 * TILE
            grads[w, r : r + 16, c : c + TILE] = gath[w, k].astype(F32)
        copies.append(pltpu.make_async_copy(grads.at[w], target, sems.at[w]))
        copies[-1].start()
    for copy in copies:
        copy.wait()


def on_device(
    features, new_owner, rim_rows, rim_counts, tile_sources, tile_values, w_self, w_neigh, cotangent
):
    rows, width = features.shape[2:]
    blocks = new_owner.shape[2]
    n_rows = cotangent.shape[2]
    hid = w_self.shape[1]
    nodes = rows * lax.axis_size("dom") * lax.axis_size("group")
    scale = 1.0 / math.sqrt(nodes)
    any_spec = pl.BlockSpec(memory_space=pl.ANY)
    out, gath = pl.pallas_call(
        functools.partial(kernel, scale),
        out_shape=(
            pltpu.VMEM((n_rows, hid), BF16),
            pltpu.VMEM((2, PIECES, 16, TILE), BF16),
        ),
        in_specs=[any_spec] * 9,
        out_specs=[any_spec] * 2,
        scratch_shapes=[
            pltpu.VMEM((rows, width), BF16),
            pltpu.VMEM((1, blocks), I32),
            pltpu.VMEM((4, TILE), I32),
            pltpu.SMEM((1, 4), I32),
            pltpu.SMEM((4, SIDE), I32),
            pltpu.VMEM((SIDE, 4, TILE, TILE), BF16),
            pltpu.VMEM((width, hid), BF16),
            pltpu.VMEM((width, hid), BF16),
            pltpu.VMEM((n_rows, hid), BF16),
            pltpu.VMEM((n_rows, hid), BF16),
            pltpu.VMEM((SIDE, TILE, width), BF16),
            pltpu.VMEM((SIDE + 4, TILE, width), BF16),
            pltpu.VMEM((4, TILE, n_rows), BF16),
            pltpu.VMEM((4, TILE, width), BF16),
            pltpu.VMEM((2, width, n_rows), BF16),
            pltpu.VMEM((n_rows, hid), F32),
            pltpu.VMEM((n_rows, width), BF16),
            pltpu.VMEM((n_rows, hid), BF16),
            pltpu.VMEM((width, hid), F32),
            pltpu.VMEM((width, hid), F32),
            pltpu.VMEM((width, hid), F32),
            pltpu.VMEM((PIECES, 16, TILE), BF16),
            pltpu.VMEM((SIDE * SIDE, 16, TILE), BF16),
            pltpu.VMEM((16, TILE), F32),
            pltpu.VMEM((SIDE, 16, TILE), F32),
            pltpu.VMEM((16, TILE), BF16),
            pltpu.SemaphoreType.DMA((9,)),
            pltpu.SemaphoreType.DMA,
            pltpu.SemaphoreType.DMA,
            pltpu.SemaphoreType.DMA,
            pltpu.SemaphoreType.DMA((4,)),
            pltpu.SemaphoreType.DMA((4,)),
            pltpu.SemaphoreType.DMA((PARTS,)),
            pltpu.SemaphoreType.DMA((PARTS,)),
            pltpu.SemaphoreType.DMA((5,)),
            pltpu.SemaphoreType.DMA((5,)),
        ],
        compiler_params=pltpu.CompilerParams(
            collective_id=0, has_side_effects=True, vmem_limit_bytes=VMEM_LIMIT
        ),
    )(
        *(
            pltpu.with_memory_space_constraint(a, pltpu.HBM)
            for a in (
                features[0, 0],
                new_owner[0, 0, :, 0][None],
                rim_rows[0, 0],
                rim_counts[0],
                tile_sources[0, 0].T,
                tile_values[0, 0],
                w_self,
                w_neigh,
                cotangent[0, 0],
            )
        )
    )
    out, g_self, g_neigh = pl.pallas_call(
        finish,
        out_shape=(
            pltpu.HBM((n_rows, hid), BF16),
            pltpu.HBM((width, hid), F32),
            pltpu.HBM((width, hid), F32),
        ),
        in_specs=[any_spec, pl.BlockSpec(memory_space=pltpu.VMEM)],
        out_specs=[any_spec] * 3,
        scratch_shapes=[pltpu.VMEM((2, width, hid), F32), pltpu.SemaphoreType.DMA((3,))],
        compiler_params=pltpu.CompilerParams(vmem_limit_bytes=VMEM_LIMIT),
    )(out, gath)
    return (out[None, None], g_self, g_neigh)


def solution(mesh):
    return jax.shard_map(
        on_device,
        mesh=mesh,
        in_specs=(
            P("group", "dom", None, None),
            P("group", "dom", None, None),
            P("group", "dom", None, None),
            P("group", "dom", None),
            P("group", "dom", None, None),
            P("group", "dom", None, None, None, None),
            P(),
            P(),
            P("group", "dom", None, None),
        ),
        out_specs=(P("group", "dom", None, None), P(), P()),
        check_vma=False,
    )
```
